32 devices in a mesh: gx: 4 (over y, x), gy: 4 (over z), gz: 2 (over core).
Axes of the slice: x: 2, y: 2, z: 4, core: 2. Of those that a mesh axis runs over, the one named last changes fastest.
Arguments:
- populations: float32 [19, 16, 64, 256], P(None, 'gx', 'gy', 'gz'), may hold values from 0.02 to 0.12
- solid: int32 [16, 64, 256], P('gx', 'gy', 'gz'), may hold values 0 or 1
- coefficients: float32 [512, 16, 256], P(('gx', 'gz')), may hold values from -0.09375 to 0.09375
- body_nodes: float32 [3, 512, 512], P(None, 'gy', ('gx', 'gz')), may hold values from -2 to 2
- centers: float32 [3, 512], P(None, ('gx', 'gz')), may hold values from -0.5 to 0.5
- angles: float32 [3, 512], P(None, ('gx', 'gz')), may hold values from -3.140625 to 3.140625
- velocity: float32 [6, 512], P(None, ('gx', 'gz')), may hold values from -0.5 to 0.5
- node_frac: float32 [3, 512, 512], P(None, 'gy', ('gx', 'gz')), may hold values from 0 to 1
- node_cell: int32 [512, 512], P('gy', ('gx', 'gz')), may hold values from 0 to 6014, as said below
- grain_tile: int32 [4, 512, 1], P('gy', ('gx', 'gz')), may hold values from 0 to 7; in each aligned block of 64 rows (0 to 63, 64 to 127, ..., all dimensions but the last counted through in order) at most 16 rows name the same one
- send_grain: int32 [8, 32], P(('gx', 'gz')), may hold values from -1 to 63, as said below
- recv_partner: int32 [8, 32], P(('gx', 'gz')), may hold values from -1 to 63, as said below
Outputs:
- populations_out: float32 [19, 16, 64, 256], P(None, 'gx', 'gy', 'gz')
- centers_out: float32 [3, 512], P(None, ('gx', 'gz'))
- velocity_out: float32 [6, 512], P(None, ('gx', 'gz'))
The draws below stay inside these ranges and needn't reach their ends.
Inputs may be any that keep to these rules, and one draw needn't show every extreme that they name: `node_cell`: c = (x * 16 + y) * 128 + z with x < 3, y < 15, z < 127, so all eight corners lie in the tile. `grain_tile`: in the rows of one device at most 16 grains name the same tile, a bound that some block reaches. `send_grain`: -1 marks an empty slot; within each destination's 4 slots the live ones come first; slot k for destination d on source s is live exactly when slot k for source s on owner d is live in recv_partner; some owner receives all 4 slots live from every source. `recv_partner`: -1 marks an empty slot, matching send_grain as stated there.
All inputs are finite; a program needn't handle non-finite values. No bound on the sum of `solid` on one device may be relied on, other than what follows from the above.
Results may differ from the reference program's by a relative error of at most 0.0001.
Values sent between devices are 32-bit elements; how exact they have to be, the bound alone decides.
A program may use at most 128 MiB of HBM per device.

```python
import math
import jax
import jax.numpy as jnp
import numpy as np
from jax import lax

Q = 19
ORDER = 16
NODES = 512
STEPS = 2
GR_OWN = 64
CX = 4
CY = 16
CZ = 128
CAP = 4
OWNERS = 8
TILES_Z = 2
GRAINS = 512
SLAB = 128
TILE_CAP = 16
NX = 16
NY = 64
NZ = 256
N_GY = 4


def contact_live(key):
    base_key = jax.random.fold_in(key, 11)
    first_key, second_key, third_key = jax.random.split(base_key, 3)
    lowest = max(1, CAP // 4)
    levels = jax.random.randint(first_key, (OWNERS,), lowest, CAP + 1)
    busiest = jax.random.randint(second_key, (), 0, OWNERS)
    is_busiest = jnp.arange(OWNERS) == busiest
    levels = jnp.where(is_busiest, CAP, levels)
    spread = levels - levels // 2 + 1
    counts = jax.random.randint(third_key, (OWNERS, OWNERS), 0, 1 << 20) % spread[None, :] + (levels // 2)[None, :]
    counts = jnp.where(is_busiest[None, :], CAP, counts)
    slots = jnp.arange(CAP)
    return slots[None, None, :] < counts[:, :, None]


def draw_send_grain(key, part):
    live = contact_live(key)
    picks = jax.random.randint(jax.random.fold_in(key, 12), (OWNERS, OWNERS, CAP), 0, GR_OWN)
    return jnp.where(live, picks, -1).reshape(OWNERS, OWNERS * CAP).astype(jnp.int32)


def draw_recv_partner(key, part):
    live = jnp.transpose(contact_live(key), (1, 0, 2))
    picks = jax.random.randint(jax.random.fold_in(key, 13), (OWNERS, OWNERS, CAP), 0, GR_OWN)
    return jnp.where(live, picks, -1).reshape(OWNERS, OWNERS * CAP).astype(jnp.int32)


def draw_node_cell(key, part):
    key_x, key_y, key_z = jax.random.split(jax.random.fold_in(key, 14), 3)
    along_x = jax.random.randint(key_x, (NODES, GRAINS), 0, CX - 1)
    along_y = jax.random.randint(key_y, (NODES, GRAINS), 0, CY - 1)
    along_z = jax.random.randint(key_z, (NODES, GRAINS), 0, CZ - 1)
    return ((along_x * CY + along_y) * CZ + along_z).astype(jnp.int32)


def touch_ends(entries, own_key, low, high):
    extent = entries.shape
    index_at = [jax.random.randint(jax.random.fold_in(own_key, axis), (), 0, extent[axis]) for axis in range(len(extent))]
    entries = entries.at[tuple(index_at)].set(low)
    longest = extent.index(max(extent))
    index_at[longest] = (index_at[longest] + 1) % extent[longest]
    return entries.at[tuple(index_at)].set(high)


def shard_levels(own_key, extent, cuts, smallest, largest):
    factor_of, own = 1.0, jax.random.fold_in(own_key, 6)
    for position, parts in cuts:
        steps = jnp.exp(jax.random.uniform(jax.random.fold_in(own, position), (parts,), jnp.float32, smallest / len(cuts), largest / len(cuts)))
        factor_of = factor_of * jnp.repeat(steps, extent[position] // parts).reshape([-1 if axis == position else 1 for axis in range(len(extent))])
    return factor_of


def deal_out(rng, own, number, rows, amount, top, most, skew):
    order = jax.random.permutation(rng, amount)
    packed, usual = shares(amount, rows * top, most, skew, True), shares(amount, rows * top, most, skew, False)
    places = jnp.arange(amount)

    def named(lengths, offset_by):
        used = int((lengths > 0).sum())
        fixed = max(1, used // 4)
        moved = fixed + (places - fixed + offset_by * (used - fixed)) % max(1, amount - fixed)
        return jnp.zeros((amount,), jnp.int32).at[order[jnp.where(places < fixed, places, moved)]].set(jnp.asarray(lengths, jnp.int32))

    lengths = jnp.where(number % 4 == 0, named(packed, number // 4), named(usual, number - number // 4 - 1))
    mixed = jax.random.permutation(jax.random.fold_in(own, 3), amount)
    giver, taker = mixed[0:amount // 2 * 2:2], mixed[1:amount // 2 * 2:2]
    margin = jnp.minimum(lengths[giver] - 1, most - lengths[taker]) // 2
    margin = jnp.where((giver == order[0]) | (taker == order[0]) | (lengths[taker] == 0), 0, jnp.maximum(margin, 0))
    moved = jax.random.randint(jax.random.fold_in(own, 4), (amount // 2,), 0, 1 << 20) % (margin + 1)
    lengths = lengths.at[giver].add(-moved).at[taker].add(moved)
    items = jnp.searchsorted(jnp.cumsum(lengths), jnp.arange(rows * top), side="right").astype(jnp.int32)
    listing = items.reshape(top, rows).T
    listing = listing[jax.random.permutation(jax.random.fold_in(own, 1), rows)]
    offset_by = jax.random.randint(jax.random.fold_in(own, 2), (rows, 1), 0, top)
    return jnp.take_along_axis(listing, (jnp.arange(top)[None, :] + offset_by) % top, axis=1)


def shares(number_of, total, bound, skew, full):
    portions = [(1 << 20) // math.isqrt(grade ** skew) + 1 for grade in range(1, number_of + 1)]
    largest = bound if full else min(bound, max(-(-total // number_of), total * portions[0] // sum(portions)))
    least = 1 if total - largest >= number_of - 1 else 0
    holding, rest = [largest] + [least] * (number_of - 1), total - largest - least * (number_of - 1)
    while rest > 0:
        candidates = [i for i in range(1, number_of) if holding[i] < largest] or [i for i in range(1, number_of) if holding[i] < bound]
        pool, remaining = sum([portions[i] for i in candidates]), rest
        for i in candidates:
            extra = min(bound - holding[i], max(1, remaining * portions[i] // pool), rest)
            holding[i] = holding[i] + extra
            rest = rest - extra
    return np.array(holding)


def noise(rng, shape, width, limit, shards=(), kind=jnp.bfloat16):
    values = width * jax.random.normal(rng, shape, jnp.float32)
    if shards:
        values = values * shard_levels(rng, shape, shards, -0.22, 0.18)
    return jnp.clip(values, -limit, limit).astype(kind)


def setup_inputs(seed: int = 0) -> dict:
    streams_of = jax.random.split(jax.random.key(seed), 13)
    populations = jnp.clip(0.02 + 0.09999999776482582 * jax.random.uniform(streams_of[0], (Q, NX, NY, NZ), jnp.float32) ** shard_levels(streams_of[0], (Q, NX, NY, NZ), ((1, 4), (2, 4), (3, 2)), -0.2, 0.2), 0.02, 0.12)
    solid = touch_ends((jax.random.randint(streams_of[1], (NX, NY, NZ), 0, 6) < 1).astype(jnp.int32), jax.random.fold_in(streams_of[1], 1), 0, 1)
    coefficients = noise(streams_of[2], (GRAINS, ORDER, ORDER * ORDER), (1.0 / (4 * ORDER)), 0.09375, ((0, 8),), jnp.float32)
    body_nodes = noise(streams_of[3], (3, NODES, GRAINS), 0.4, 2.0, ((1, 4), (2, 8)), jnp.float32)
    centers = jnp.clip(jax.random.uniform(streams_of[4], (3, GRAINS), jnp.float32, -0.5, 0.5) * shard_levels(streams_of[4], (3, GRAINS), ((1, 8),), -0.4, 0.0), -0.5, 0.5)
    angles = jnp.clip(jax.random.uniform(streams_of[5], (3, GRAINS), jnp.float32, -3.140625, 3.140625), -3.140625, 3.140625)
    velocity = noise(streams_of[6], (6, GRAINS), 0.1, 0.5, ((1, 8),), jnp.float32)
    node_frac = jnp.clip(1.0 * jax.random.uniform(streams_of[7], (3, NODES, GRAINS), jnp.float32) ** shard_levels(streams_of[7], (3, NODES, GRAINS), ((1, 4), (2, 8)), -0.2, 0.2), 0.0, 1.0)
    node_cell = draw_node_cell(jax.random.fold_in(streams_of[12], 71), 0)
    grain_tile_keys = jax.random.split(jax.random.fold_in(streams_of[9], 1), N_GY * GRAINS // GR_OWN)
    grain_tile_turns = jax.random.permutation(jax.random.fold_in(streams_of[9], 3), N_GY * GRAINS // GR_OWN)
    grain_tile = jax.vmap(lambda own, number: deal_out(jax.random.fold_in(streams_of[9], 2), own, number, GR_OWN, OWNERS, 1, TILE_CAP, 2))(grain_tile_keys, grain_tile_turns).reshape((N_GY, GRAINS, 1))
    send_grain = draw_send_grain(jax.random.fold_in(streams_of[12], 71), 0)
    recv_partner = draw_recv_partner(jax.random.fold_in(streams_of[12], 71), 0)
    return dict(populations=populations, solid=solid, coefficients=coefficients, body_nodes=body_nodes, centers=centers, angles=angles, velocity=velocity, node_frac=node_frac, node_cell=node_cell, grain_tile=grain_tile, send_grain=send_grain, recv_partner=recv_partner)


highest = lax.Precision.HIGHEST
lattice_dirs = np.array([[0, 0, 0], [1, 0, 0], [-1, 0, 0], [0, 1, 0], [0, -1, 0], [0, 0, 1], [0, 0, -1], [1, 1, 0], [-1, -1, 0], [1, -1, 0], [-1, 1, 0], [1, 0, 1], [-1, 0, -1], [1, 0, -1], [-1, 0, 1], [0, 1, 1], [0, -1, -1], [0, 1, -1], [0, -1, 1]], dtype=np.int32)
lattice_float = lattice_dirs.astype(np.float32)
lattice_weights = np.array([1.0 / 3.0] + [1.0 / 18.0] * 6 + [1.0 / 36.0] * 12, dtype=np.float32)
opposite_dirs = np.array([0, 2, 1, 4, 3, 6, 5, 8, 7, 10, 9, 12, 11, 14, 13, 16, 15, 18, 17], dtype=np.int32)
tau_relax = 0.9
ib_stiffness = 0.5
contact_stiffness = 0.05
time_step = 0.05

def compose(left, right):
    return jnp.einsum('ijg,jkg->ikg', left, right, precision=highest)

def cross_product(left, right):
    return jnp.stack([left[1] * right[2] - left[2] * right[1], left[2] * right[0] - left[0] * right[2], left[0] * right[1] - left[1] * right[0]])

def rotation_from(angles):
    cosine_a, sine_a = (jnp.cos(angles[0]), jnp.sin(angles[0]))
    cosine_b, sine_b = (jnp.cos(angles[1]), jnp.sin(angles[1]))
    cosine_c, sine_c = (jnp.cos(angles[2]), jnp.sin(angles[2]))
    unit = jnp.ones_like(cosine_a)
    empty = jnp.zeros_like(cosine_a)
    about_x = jnp.stack([jnp.stack([unit, empty, empty]), jnp.stack([empty, cosine_a, -sine_a]), jnp.stack([empty, sine_a, cosine_a])])
    about_y = jnp.stack([jnp.stack([cosine_b, empty, sine_b]), jnp.stack([empty, unit, empty]), jnp.stack([-sine_b, empty, cosine_b])])
    about_z = jnp.stack([jnp.stack([cosine_c, -sine_c, empty]), jnp.stack([sine_c, cosine_c, empty]), jnp.stack([empty, empty, unit])])
    return compose(about_z, compose(about_y, about_x))

def chebyshev(coords, order):
    first_kind = [jnp.ones_like(coords), coords]
    second_kind = [jnp.ones_like(coords), 2.0 * coords]
    for degree in range(2, order):
        first_kind.append(2.0 * coords * first_kind[-1] - first_kind[-2])
        second_kind.append(2.0 * coords * second_kind[-1] - second_kind[-2])
    slopes = [jnp.zeros_like(coords)] + [degree * second_kind[degree - 1] for degree in range(1, order)]
    return (jnp.stack(first_kind[:order]), jnp.stack(slopes))

def contact_forces(coefs, rotation, centre, nodes):
    order = coefs.shape[1]
    count = nodes.shape[1]
    pieces = coefs.shape[0]
    relative = nodes - centre[:, None, :]
    local = jnp.clip(jnp.einsum('jib,jnb->inb', rotation, relative, precision=highest), -1.0, 1.0)
    poly_x, slope_x = chebyshev(local[0], order)
    poly_y, slope_y = chebyshev(local[1], order)
    poly_z, slope_z = chebyshev(local[2], order)
    along_z = jnp.concatenate([poly_z, slope_z], axis=1)
    table = coefs.reshape(pieces, order * order, order)
    partial_sum = jnp.einsum('brc,cmb->rmb', table, along_z, precision=highest).reshape(order, order, 2 * count, pieces)
    value_part = jnp.einsum('abnk,bnk->ank', partial_sum[:, :, :count], poly_y, precision=highest)
    slope_zpart = jnp.einsum('abnk,bnk->ank', partial_sum[:, :, count:], poly_y, precision=highest)
    slope_ypart = jnp.einsum('abnk,bnk->ank', partial_sum[:, :, :count], slope_y, precision=highest)
    level = lax.optimization_barrier(jnp.sum(value_part * poly_x, axis=0))
    gradient = jnp.stack([lax.optimization_barrier(jnp.sum(value_part * slope_x, axis=0)), lax.optimization_barrier(jnp.sum(slope_ypart * poly_x, axis=0)), lax.optimization_barrier(jnp.sum(slope_zpart * poly_x, axis=0))])
    depth = jnp.maximum(-level, 0.0)
    strength = contact_stiffness * depth / jnp.sqrt(1.0 + lax.optimization_barrier(jnp.sum(gradient * gradient, axis=0)))
    return jnp.einsum('ijb,jnb->inb', rotation, gradient, precision=highest) * strength[None]

def moments(flat):
    density = lax.optimization_barrier(jnp.sum(flat, axis=0))
    momentum = jnp.einsum('qa,qc->ac', lattice_float, flat, precision=highest)
    return (density, momentum / density[None])

def collide(flat, density, fluid_velocity, force, solid_flat):
    shifted = fluid_velocity + tau_relax * force / density[None]
    along = jnp.einsum('qa,ac->qc', lattice_float, shifted, precision=highest)
    speed = lax.optimization_barrier(jnp.sum(shifted * shifted, axis=0))
    balance = lattice_weights[:, None] * density[None] * (1.0 + 3.0 * along + 4.5 * along * along - 1.5 * speed[None])
    relaxed = flat - (flat - balance) / tau_relax
    return jnp.where(solid_flat[None] > 0, flat, relaxed)

def corner_terms(frac, base, stride_x, stride_y):
    terms = []
    for offset_x in (0, 1):
        weight_x = frac[0] if offset_x else 1.0 - frac[0]
        for offset_y in (0, 1):
            weight_y = frac[1] if offset_y else 1.0 - frac[1]
            for offset_z in (0, 1):
                weight_z = frac[2] if offset_z else 1.0 - frac[2]
                terms.append((base + offset_x * stride_x + offset_y * stride_y + offset_z, weight_x * weight_y * weight_z))
    return terms

def advance(centre, motion, rotation, totals):
    motion = motion + time_step * totals
    centre = centre + time_step * motion[0:3]
    spin = motion[3:6]
    empty = jnp.zeros_like(spin[0])
    skew = jnp.stack([jnp.stack([empty, -spin[2], spin[1]]), jnp.stack([spin[2], empty, -spin[0]]), jnp.stack([-spin[1], spin[0], empty])])
    rotation = rotation + time_step * compose(skew, rotation)
    return (centre, motion, rotation)

def reference(populations, solid, coefficients, body_nodes, centers, angles, velocity, node_frac, node_cell, grain_tile, send_grain, recv_partner):
    owners = OWNERS
    grains = GRAINS
    sends = jnp.transpose(send_grain.reshape(owners, owners, CAP), (1, 0, 2))
    recvs = recv_partner.reshape(owners, owners, CAP)
    source = jnp.broadcast_to(jnp.arange(owners, dtype=jnp.int32)[None, :, None], recvs.shape)
    target = jnp.broadcast_to(jnp.arange(owners, dtype=jnp.int32)[:, None, None], recvs.shape)
    alive_all = (recvs >= 0).reshape(-1).astype(jnp.float32)
    partner = (source * GR_OWN + jnp.maximum(sends, 0)).reshape(-1).astype(jnp.int32)
    holder = (target * GR_OWN + jnp.maximum(recvs, 0)).reshape(-1).astype(jnp.int32)
    pairs = owners * owners * CAP
    block = math.gcd(pairs, 8)
    dest_node = jnp.repeat(grain_tile[:, :, 0], SLAB, axis=0)
    tile_x = dest_node // TILES_Z
    tile_z = dest_node % TILES_Z
    tile_y = (jnp.arange(NODES, dtype=jnp.int32) // SLAB)[:, None]
    local_x = node_cell // (CY * CZ)
    local_y = node_cell // CZ % CY
    local_z = node_cell % CZ
    base = ((tile_x * CX + local_x) * NY + tile_y * CY + local_y) * NZ + tile_z * CZ + local_z
    corners = corner_terms(node_frac, base, NY * NZ, NZ)
    solid_flat = solid.reshape(-1)
    rotation = rotation_from(angles)
    centre = centers
    motion = velocity
    fluid = populations
    for step in range(STEPS):
        arm = jnp.einsum('ijg,jng->ing', rotation, body_nodes, precision=highest)
        positions = centre[:, None, :] + arm
        node_speed = motion[0:3, None, :] + cross_product(motion[3:6, None, :], arm)

        def pair_block(start):
            hold = lax.dynamic_slice_in_dim(holder, start, block)
            part = lax.dynamic_slice_in_dim(partner, start, block)
            alive = lax.dynamic_slice_in_dim(alive_all, start, block)
            nodes = positions[:, :, part]
            forces = contact_forces(coefficients[hold], rotation[:, :, hold], centre[:, hold], nodes) * alive[None, None, :]
            on_holder = jnp.concatenate([-lax.optimization_barrier(jnp.sum(forces, axis=1)), lax.optimization_barrier(jnp.sum(cross_product(nodes - centre[:, hold][:, None, :], -forces), axis=1))])
            on_partner = jnp.concatenate([lax.optimization_barrier(jnp.sum(forces, axis=1)), lax.optimization_barrier(jnp.sum(cross_product(nodes - centre[:, part][:, None, :], forces), axis=1))])
            return (on_holder, on_partner)
        holder_terms, partner_terms = lax.map(pair_block, jnp.arange(0, pairs, block, dtype=jnp.int32))
        holder_terms = jnp.moveaxis(holder_terms, 1, 0).reshape(6, pairs)
        partner_terms = jnp.moveaxis(partner_terms, 1, 0).reshape(6, pairs)
        loads = jax.ops.segment_sum(holder_terms.T, holder, num_segments=grains).T + jax.ops.segment_sum(partner_terms.T, partner, num_segments=grains).T
        flat = fluid.reshape(Q, NX * NY * NZ)
        density, fluid_velocity = moments(flat)
        interp = jnp.zeros(node_speed.shape, jnp.float32)
        for index, weight in corners:
            interp = interp + weight[None] * fluid_velocity[:, index]
        node_force = ib_stiffness * (node_speed - interp)
        cell_force = jnp.zeros((3, NX * NY * NZ), jnp.float32)
        for index, weight in corners:
            cell_force = cell_force.at[:, index].add(weight[None] * node_force)
        totals = loads + jnp.concatenate([-lax.optimization_barrier(jnp.sum(node_force, axis=1)), lax.optimization_barrier(jnp.sum(cross_product(arm, -node_force), axis=1))])
        post = collide(flat, density, fluid_velocity, cell_force, solid_flat).reshape(Q, NX, NY, NZ)
        moved = jnp.stack([jnp.roll(post[direction], shift=tuple((int(value) for value in lattice_dirs[direction])), axis=(0, 1, 2)) for direction in range(Q)])
        fluid = jnp.where(solid[None] > 0, moved[opposite_dirs], moved)
        centre, motion, rotation = advance(centre, motion, rotation, totals)
    return (fluid, centre, motion)
```

```python
import functools
import math

import jax
import jax.numpy as jnp
import numpy as np
from jax import lax
from jax.experimental import pallas as pl
from jax.experimental.pallas import tpu as pltpu
from jax.sharding import PartitionSpec as P

STEPS = 2

highest = lax.Precision.HIGHEST
lattice_dirs = np.array(
    [
        [0, 0, 0],
        [1, 0, 0],
        [-1, 0, 0],
        [0, 1, 0],
        [0, -1, 0],
        [0, 0, 1],
        [0, 0, -1],
        [1, 1, 0],
        [-1, -1, 0],
        [1, -1, 0],
        [-1, 1, 0],
        [1, 0, 1],
        [-1, 0, -1],
        [1, 0, -1],
        [-1, 0, 1],
        [0, 1, 1],
        [0, -1, -1],
        [0, 1, -1],
        [0, -1, 1],
    ],
    dtype=np.int32,
)
lattice_weights = [1.0 / 3.0] + [1.0 / 18.0] * 6 + [1.0 / 36.0] * 12
opposite_dirs = np.array(
    [0, 2, 1, 4, 3, 6, 5, 8, 7, 10, 9, 12, 11, 14, 13, 16, 15, 18, 17], dtype=np.int32
)
tau_relax = 0.9
ib_stiffness = 0.5
contact_stiffness = 0.05
time_step = 0.05
bf16 = jnp.bfloat16
f32 = jnp.float32


def padded_2(cells, sides, width):
    for axis, dim in sides:
        count = lax.axis_size(axis)
        head = lax.slice_in_dim(cells, 0, width, axis=dim)
        tail = lax.slice_in_dim(cells, cells.shape[dim] - width, cells.shape[dim], axis=dim)
        cells = jnp.concatenate(
            [
                lax.ppermute(tail, axis, [(i, (i + 1) % count) for i in range(count)]),
                cells,
                lax.ppermute(head, axis, [((i + 1) % count, i) for i in range(count)]),
            ],
            axis=dim,
        )
    return cells


def stream(post, solid):
    directions = post.shape[0]
    moved = post
    for axis_part, axis in enumerate(("gx", "gy", "gz")):
        chosen = [d for d in range(directions) if lattice_dirs[d][axis_part] != 0]
        selected = moved[np.array(chosen, dtype=np.int32)]
        padded = padded_2(selected, ((axis, axis_part + 1),), 1)
        extent = selected.shape[axis_part + 1]
        shifted = [
            lax.slice_in_dim(
                padded[position],
                1 - int(lattice_dirs[direction][axis_part]),
                1 - int(lattice_dirs[direction][axis_part]) + extent,
                axis=axis_part,
            )
            for position, direction in enumerate(chosen)
        ]
        moved = moved.at[np.array(chosen, dtype=np.int32)].set(jnp.stack(shifted))
    return jnp.where(solid[None] > 0, moved[opposite_dirs], moved)


def rotation_rows(angles):
    ca, sa = jnp.cos(angles[0]), jnp.sin(angles[0])
    cb, sb = jnp.cos(angles[1]), jnp.sin(angles[1])
    cc, sc = jnp.cos(angles[2]), jnp.sin(angles[2])
    return [
        cc * cb,
        cc * sb * sa - sc * ca,
        cc * sb * ca + sc * sa,
        sc * cb,
        sc * sb * sa + cc * ca,
        sc * sb * ca - cc * sa,
        -sb,
        cb * sa,
        cb * ca,
    ]


def advance_rows(rows, totals):
    rotation, centre, motion = rows[0:9], rows[9:12], rows[12:18]
    motion = [motion[i] + time_step * totals[i] for i in range(6)]
    centre = [centre[i] + time_step * motion[i] for i in range(3)]
    spin = motion[3:6]
    turned = []
    for i in range(3):
        j, k = (i + 1) % 3, (i + 2) % 3
        for c in range(3):
            cross = spin[j] * rotation[3 * k + c] - spin[k] * rotation[3 * j + c]
            turned.append(rotation[3 * i + c] + time_step * cross)
    return turned + centre + motion


def cross(left, right):
    return [
        left[1] * right[2] - left[2] * right[1],
        left[2] * right[0] - left[0] * right[2],
        left[0] * right[1] - left[1] * right[0],
    ]


def split(values):
    high = values.astype(bf16)
    return high, (values - high.astype(f32)).astype(bf16)


def pack_kernel(index_ref, name_ref, tiles_ref, out_ref):
    row = lax.broadcasted_iota(jnp.int32, tiles_ref.shape[1:], 0)

    def body(slot, carry):
        tile = tiles_ref[index_ref[slot]]
        out_ref[slot] = jnp.where(row == 7, name_ref[slot], tile)
        return carry

    lax.fori_loop(0, out_ref.shape[0], body, 0, unroll=8)


def pack(index, name, tiles):
    return pl.pallas_call(
        pack_kernel,
        out_shape=jax.ShapeDtypeStruct((index.shape[0],) + tiles.shape[1:], f32),
        in_specs=[
            pl.BlockSpec(memory_space=pltpu.SMEM),
            pl.BlockSpec(memory_space=pltpu.SMEM),
            pl.BlockSpec(memory_space=pltpu.VMEM),
        ],
        out_specs=pl.BlockSpec(memory_space=pltpu.VMEM),
    )(index, name, tiles)


def columns(matrix, count):
    return [matrix[:, i : i + 1] for i in range(count)]


def lane_pack(values):
    rows = values[0].shape[0]
    lane = lax.broadcasted_iota(jnp.int32, (rows, 128), 1)
    out = jnp.zeros((rows, 128), f32)
    for i, value in enumerate(values):
        out = jnp.where(lane == i, value, out)
    return out


def total(values):
    return jnp.sum(values, axis=1, keepdims=True)


def step_kernel(
    size_y,
    tile_cap,
    chunk,
    counts_ref,
    pick_ref,
    state_ref,
    slots_ref,
    contacts_ref,
    holder_ref,
    coef_ref,
    fluid_ref,
    solid_ref,
    post_ref,
    loads_ref,
    poly_ref,
    level_ref,
    grid_ref,
    speed_ref,
    force_ref,
    cell_ref,
    velocity_ref,
):
    state = state_ref[...]
    grains = state.shape[1]
    tile_slots, _, nodes = slots_ref.shape
    contact_slots = contacts_ref.shape[0]
    order = coef_ref.shape[1]
    directions, plane, size_z = fluid_ref.shape
    size_x = plane // size_y

    def one_hot(ids):
        lane = lax.broadcasted_iota(jnp.int32, (ids.shape[0], grains), 1).astype(f32)
        return jnp.where(lane == ids, 1.0, 0.0)

    def picked(hot):
        found = lax.dot_general(
            hot, state, (((1,), (1,)), ((), ())), precision=highest, preferred_element_type=f32
        )
        return columns(found, 18)

    def gathered(values, hot):
        return lax.dot_general(
            lane_pack(values), hot, (((0,), (0,)), ((), ())), precision=highest, preferred_element_type=f32
        )[0:8]

    partner_hot = one_hot(contacts_ref[:, 7, :][:, 0:1])
    holder_hot = one_hot(holder_ref[...])
    partner = picked(partner_hot)
    holder = picked(holder_hot)
    alive = jnp.where(holder_ref[...] >= 0.0, 1.0, 0.0)
    body = [contacts_ref[:, i, :] for i in range(3)]
    arm = [
        partner[3 * i] * body[0] + partner[3 * i + 1] * body[1] + partner[3 * i + 2] * body[2]
        for i in range(3)
    ]
    rel = [(partner[9 + i] + arm[i]) - holder[9 + i] for i in range(3)]
    for d in range(3):
        y = jnp.clip(holder[d] * rel[0] + holder[3 + d] * rel[1] + holder[6 + d] * rel[2], -1.0, 1.0)
        first = [jnp.ones_like(y), y]
        second = [jnp.ones_like(y), 2.0 * y]
        for degree in range(2, order):
            first.append(2.0 * y * first[-1] - first[-2])
            second.append(2.0 * y * second[-1] - second[-2])
        for degree in range(order):
            slope = degree * second[degree - 1] if degree else jnp.zeros_like(y)
            poly_ref[2 * d, :, degree, :] = first[degree]
            poly_ref[2 * d + 1, :, degree, :] = slope

    def contact(slot, carry):
        high, low = split(coef_ref[pick_ref[slot]])
        table = jnp.concatenate([high, low, high], axis=0)
        along = jnp.concatenate([poly_ref[0, slot], poly_ref[1, slot]], axis=1)
        along_high, along_low = split(along)
        along = jnp.concatenate([along_high, along_high, along_low], axis=0)
        part = lax.dot_general(table, along, (((0,), (0,)), ((), ())), preferred_element_type=f32)
        poly_y, slope_y = poly_ref[2, slot], poly_ref[3, slot]
        poly_z, slope_z = poly_ref[4, slot], poly_ref[5, slot]
        value = slope_xp = slope_yp = None
        for b in range(order):
            here = part[b * order : (b + 1) * order, 0:nodes]
            there = part[b * order : (b + 1) * order, nodes : 2 * nodes]
            t, s = poly_y[b : b + 1], slope_y[b : b + 1]
            if b == 0:
                value, slope_xp, slope_yp = here * t, there * t, here * s
            else:
                value, slope_xp, slope_yp = value + here * t, slope_xp + there * t, slope_yp + here * s
        for i, terms in enumerate((value * poly_z, slope_xp * poly_z, slope_yp * poly_z, value * slope_z)):
            level_ref[i, pl.ds(slot, 1), :] = jnp.sum(terms, axis=0, keepdims=True)
        return carry

    lax.fori_loop(0, contact_slots, contact, 0, unroll=math.gcd(contact_slots, 4))

    gradient = [level_ref[i + 1] for i in range(3)]
    depth = jnp.maximum(-level_ref[0], 0.0)
    norm = gradient[0] * gradient[0] + gradient[1] * gradient[1] + gradient[2] * gradient[2]
    strength = contact_stiffness * depth / jnp.sqrt(1.0 + norm) * alive
    push = [
        (holder[3 * i] * gradient[0] + holder[3 * i + 1] * gradient[1] + holder[3 * i + 2] * gradient[2])
        * strength
        for i in range(3)
    ]
    sums = [total(push[i]) for i in range(3)]
    on_holder = [-s for s in sums] + [-total(t) for t in cross(rel, push)]
    on_partner = sums + [total(t) for t in cross(arm, push)]
    loads = gathered(on_holder, holder_hot) + gathered(on_partner, partner_hot)

    density = fluid_ref[0]
    momentum = [None, None, None]
    for q in range(1, directions):
        values = fluid_ref[q]
        density = density + values
        for i in range(3):
            e = int(lattice_dirs[q][i])
            if e:
                term = values if e > 0 else -values
                momentum[i] = term if momentum[i] is None else momentum[i] + term
    inverse = 1.0 / density
    for i in range(3):
        flow = momentum[i] * inverse
        velocity_ref[i] = flow
        high, low = split(flow)
        rows = pl.ds(i * plane, plane)
        grid_ref[rows, 0:size_z] = high
        grid_ref[rows, size_z : 2 * size_z] = low
        grid_ref[rows, 2 * size_z : 3 * size_z] = high

    slot_hot = one_hot(slots_ref[:, 7, :][:, 0:1])
    own = picked(slot_hot)
    body = [slots_ref[:, i, :] for i in range(3)]
    arm = [own[3 * i] * body[0] + own[3 * i + 1] * body[1] + own[3 * i + 2] * body[2] for i in range(3)]
    swirl = cross(own[15:18], arm)
    for i in range(3):
        speed_ref[:, i, :] = own[12 + i] + swirl[i]
    force_ref[...] = jnp.zeros_like(force_ref)
    cell_ref[...] = jnp.zeros_like(cell_ref)
    depth_row = lax.broadcasted_iota(jnp.int32, (size_z, nodes), 0).astype(f32)
    y_row = lax.broadcasted_iota(jnp.int32, (size_y, nodes), 0).astype(f32)

    def spread(start):
        highs, lows, plane_weights = [], [], []
        for k in range(chunk):
            tile = slots_ref[start + k]
            cell = tile[6:7]
            line = jnp.floor((cell + 0.5) * (1.0 / size_z))
            base_z = cell - line * size_z
            base_x = jnp.floor((line + 0.5) * (1.0 / size_y))
            base_y = line - base_x * size_y
            upper, lower = tile[5:6], 1.0 - tile[5:6]
            upper_high = upper.astype(bf16).astype(f32)
            lower_high = lower.astype(bf16).astype(f32)
            at_low, at_high = depth_row == base_z, depth_row == base_z + 1.0
            highs.append(
                jnp.where(at_low, lower_high, jnp.where(at_high, upper_high, 0.0)).astype(bf16)
            )
            lows.append(
                jnp.where(
                    at_low, lower - lower_high, jnp.where(at_high, upper - upper_high, 0.0)
                ).astype(bf16)
            )
            frac_y = tile[4:5]
            weight_y = jnp.where(
                y_row == base_y, 1.0 - frac_y, jnp.where(y_row == base_y + 1.0, frac_y, 0.0)
            )
            frac_x = tile[3:4]
            rows = []
            for x in range(size_x):
                weight_x = jnp.where(
                    base_x == float(x), 1.0 - frac_x, jnp.where(base_x == float(x - 1), frac_x, 0.0)
                )
                rows.append(weight_x * weight_y)
            plane_weights.append(jnp.concatenate(rows, axis=0))
        high = jnp.concatenate(highs, axis=1)
        low = jnp.concatenate(lows, axis=1)
        lines = jnp.dot(
            grid_ref[...], jnp.concatenate([high, high, low], axis=0), preferred_element_type=f32
        )
        spread_high, spread_low = [], []
        for k in range(chunk):
            weights = plane_weights[k]
            live = jnp.where(slots_ref[start + k][7:8] >= 0.0, ib_stiffness, 0.0)
            speed = speed_ref[start + k]
            pieces, forces = [], []
            for i in range(3):
                taken = lines[i * plane : (i + 1) * plane, k * nodes : (k + 1) * nodes]
                interp = jnp.sum(taken * weights, axis=0, keepdims=True)
                node = live * (speed[i : i + 1] - interp)
                force_ref[start + k, i : i + 1, :] = node
                pieces.append(node * weights)
            piece_high, piece_low = split(jnp.concatenate(pieces, axis=0))
            spread_high.append(piece_high)
            spread_low.append(piece_low)
        contract = (((1,), (1,)), ((), ()))
        wide = lax.dot_general(
            jnp.concatenate(spread_high, axis=1),
            jnp.concatenate([high, low], axis=0),
            contract,
            preferred_element_type=f32,
        )
        narrow = lax.dot_general(
            jnp.concatenate(spread_low, axis=1), high, contract, preferred_element_type=f32
        )
        cell_ref[...] += wide[:, 0:size_z] + wide[:, size_z : 2 * size_z] + narrow

    for source in range(tile_slots // tile_cap):

        def body_of(turn, carry, source=source):
            spread(source * tile_cap + turn * chunk)
            return carry

        lax.fori_loop(0, (counts_ref[source] + chunk - 1) // chunk, body_of, 0)

    node = [force_ref[:, i, :] for i in range(3)]
    back = [-total(node[i]) for i in range(3)] + [-total(t) for t in cross(arm, node)]
    loads_ref[...] = loads + gathered(back, slot_hot)

    for x in range(size_x):
        rows = slice(x * size_y, (x + 1) * size_y)
        density = fluid_ref[0, rows]
        for q in range(1, directions):
            density = density + fluid_ref[q, rows]
        scale = tau_relax / density
        shifted = [
            velocity_ref[i, rows] + scale * cell_ref[i * plane + x * size_y : i * plane + (x + 1) * size_y, :]
            for i in range(3)
        ]
        speed = shifted[0] * shifted[0] + shifted[1] * shifted[1] + shifted[2] * shifted[2]
        base = 1.0 - 1.5 * speed
        wall = solid_ref[rows] > 0
        for q in range(directions):
            flat = fluid_ref[q, rows]
            along = None
            for i in range(3):
                e = int(lattice_dirs[q][i])
                if e:
                    term = shifted[i] if e > 0 else -shifted[i]
                    along = term if along is None else along + term
            inside = base if along is None else base + along * (3.0 + 4.5 * along)
            balance = lattice_weights[q] * density * inside
            relaxed = flat - (flat - balance) * (1.0 / tau_relax)
            post_ref[q, rows] = jnp.where(wall, flat, relaxed)


def run_step(size_y, tile_cap, counts, pick, state, slots, contacts, holder, coefs, fluid, solid):
    grains = state.shape[1]
    tile_slots, _, nodes = slots.shape
    contact_slots = contacts.shape[0]
    order = coefs.shape[1]
    directions, plane, size_z = fluid.shape
    vmem = pl.BlockSpec(memory_space=pltpu.VMEM)
    smem = pl.BlockSpec(memory_space=pltpu.SMEM)
    return pl.pallas_call(
        functools.partial(step_kernel, size_y, tile_cap, math.gcd(tile_cap, 4)),
        out_shape=(
            jax.ShapeDtypeStruct(fluid.shape, f32),
            jax.ShapeDtypeStruct((8, grains), f32),
        ),
        in_specs=[smem, smem] + [vmem] * 7,
        out_specs=(vmem, vmem),
        scratch_shapes=[
            pltpu.VMEM((6, contact_slots, order, nodes), f32),
            pltpu.VMEM((4, contact_slots, nodes), f32),
            pltpu.VMEM((3 * plane, 3 * size_z), bf16),
            pltpu.VMEM((tile_slots, 8, nodes), f32),
            pltpu.VMEM((tile_slots, 8, nodes), f32),
            pltpu.VMEM((3 * plane, size_z), f32),
            pltpu.VMEM((3, plane, size_z), f32),
        ],
        compiler_params=pltpu.CompilerParams(vmem_limit_bytes=40 * 1024 * 1024),
    )(counts, pick, state, slots, contacts, holder, coefs, fluid, solid)


def per_device(
    populations,
    solid,
    coefficients,
    body_nodes,
    centers,
    angles,
    velocity,
    node_frac,
    node_cell,
    grain_tile,
    send_grain,
    recv_partner,
):
    directions, size_x, size_y, size_z = populations.shape
    plane = size_x * size_y
    grains = centers.shape[1]
    nodes = body_nodes.shape[1]
    count_z = lax.axis_size("gz")
    owners = lax.axis_size("gx") * count_z
    tile_cap = max(2, 2 * grains // owners)
    tile_slots = owners * tile_cap
    contact_slots = send_grain.shape[1]
    contact_cap = contact_slots // owners
    me = lax.axis_index("gx") * count_z + lax.axis_index("gz")
    first = (me * grains).astype(f32)

    route = grain_tile[0, :, 0]
    hot = (route[:, None] == jnp.arange(owners, dtype=jnp.int32)[None, :]).astype(jnp.int32)
    below = np.tril(np.ones((grains, grains), np.int32), -1)
    earlier = (route[:, None] == route[None, :]) & (below > 0)
    rank = jnp.sum(earlier.astype(jnp.int32), axis=1)
    slot_of = route * tile_cap + rank
    match = slot_of[:, None] == jnp.arange(tile_slots, dtype=jnp.int32)[None, :]
    grain_ids = jnp.arange(grains, dtype=jnp.int32)
    slot_grain = jnp.sum(jnp.where(match, grain_ids[:, None] + 1, 0), axis=0) - 1
    chosen = jnp.concatenate(
        [slot_grain.reshape(owners, tile_cap), send_grain[0].reshape(owners, contact_cap)], axis=1
    ).reshape(-1)
    name = jnp.where(chosen >= 0, chosen.astype(f32) + first, -1.0)
    tiles = jnp.concatenate(
        [body_nodes, node_frac, node_cell.astype(f32)[None], jnp.zeros((1, nodes, grains), f32)]
    ).transpose(2, 0, 1)
    packed = pack(jnp.maximum(chosen, 0), name, tiles).reshape(owners, tile_cap + contact_cap, 8, nodes)
    small = jnp.concatenate([angles, centers, velocity]).reshape(-1)
    tile_size = 8 * nodes
    small_tiles = -(-small.shape[0] // tile_size)
    small = jnp.pad(small, (0, small_tiles * tile_size - small.shape[0])).reshape(1, small_tiles, 8, nodes)
    small = jnp.broadcast_to(small, (owners, small_tiles, 8, nodes))
    got = lax.all_to_all(
        jnp.concatenate([packed, small], axis=1), ("gx", "gz"), split_axis=0, concat_axis=0, tiled=True
    )
    slots = got[:, :tile_cap].reshape(tile_slots, 8, nodes)
    contacts = got[:, tile_cap : tile_cap + contact_cap].reshape(contact_slots, 8, nodes)
    everyone = got[:, tile_cap + contact_cap :].reshape(owners, -1)[:, : 12 * grains]
    everyone = everyone.reshape(owners, 12, grains).transpose(1, 0, 2).reshape(12, owners * grains)
    counts = jnp.sum((slots[:, 7, 0].reshape(owners, tile_cap) >= 0.0).astype(jnp.int32), axis=1)
    recv = recv_partner[0]
    pick = jnp.maximum(recv, 0)
    holder = jnp.where(recv >= 0, recv.astype(f32) + first, -1.0)[:, None]

    rows = rotation_rows(everyone[0:3]) + [everyone[3 + i] for i in range(9)]
    state = jnp.stack(rows)
    solid_flat = solid.reshape(plane, size_z)
    fluid = populations
    for step in range(STEPS):
        post, loads = run_step(
            size_y,
            tile_cap,
            counts,
            pick,
            state,
            slots,
            contacts,
            holder,
            coefficients,
            fluid.reshape(directions, plane, size_z),
            solid_flat,
        )
        totals = lax.psum(loads, ("gx", "gy", "gz"))
        fluid = stream(post.reshape(populations.shape), solid)
        if step == STEPS - 1:
            state = lax.dynamic_slice_in_dim(state, me * grains, grains, axis=1)
            totals = lax.dynamic_slice_in_dim(totals, me * grains, grains, axis=1)
        state = jnp.stack(advance_rows([state[i] for i in range(18)], [totals[i] for i in range(6)]))
    return (fluid, state[9:12], state[12:18])


def solution(mesh):
    in_specs = (
        P(None, "gx", "gy", "gz"),
        P("gx", "gy", "gz"),
        P(("gx", "gz"), None, None),
        P(None, "gy", ("gx", "gz")),
        P(None, ("gx", "gz")),
        P(None, ("gx", "gz")),
        P(None, ("gx", "gz")),
        P(None, "gy", ("gx", "gz")),
        P("gy", ("gx", "gz")),
        P("gy", ("gx", "gz"), None),
        P(("gx", "gz"), None),
        P(("gx", "gz"), None),
    )
    out_specs = (P(None, "gx", "gy", "gz"), P(None, ("gx", "gz")), P(None, ("gx", "gz")))
    return jax.shard_map(
        per_device, mesh=mesh, in_specs=in_specs, out_specs=out_specs, check_vma=False
    )
```

```python
import functools
import math

import jax
import jax.numpy as jnp
import numpy as np
from jax import lax
from jax.experimental import pallas as pl
from jax.experimental.pallas import tpu as pltpu
from jax.sharding import PartitionSpec as P

STEPS = 2

highest = lax.Precision.HIGHEST
lattice_dirs = np.array(
    [
        [0, 0, 0],
        [1, 0, 0],
        [-1, 0, 0],
        [0, 1, 0],
        [0, -1, 0],
        [0, 0, 1],
        [0, 0, -1],
        [1, 1, 0],
        [-1, -1, 0],
        [1, -1, 0],
        [-1, 1, 0],
        [1, 0, 1],
        [-1, 0, -1],
        [1, 0, -1],
        [-1, 0, 1],
        [0, 1, 1],
        [0, -1, -1],
        [0, 1, -1],
        [0, -1, 1],
    ],
    dtype=np.int32,
)
lattice_weights = [1.0 / 3.0] + [1.0 / 18.0] * 6 + [1.0 / 36.0] * 12
tau_relax = 0.9
ib_stiffness = 0.5
contact_stiffness = 0.05
time_step = 0.05
bf16 = jnp.bfloat16
f32 = jnp.float32
MESH = pl.DeviceIdType.MESH


def rotation_rows(angles):
    ca, sa = jnp.cos(angles[0]), jnp.sin(angles[0])
    cb, sb = jnp.cos(angles[1]), jnp.sin(angles[1])
    cc, sc = jnp.cos(angles[2]), jnp.sin(angles[2])
    return [
        cc * cb,
        cc * sb * sa - sc * ca,
        cc * sb * ca + sc * sa,
        sc * cb,
        sc * sb * sa + cc * ca,
        sc * sb * ca - cc * sa,
        -sb,
        cb * sa,
        cb * ca,
    ]


def advance_rows(rows, totals):
    rotation, centre, motion = rows[0:9], rows[9:12], rows[12:18]
    motion = [motion[i] + time_step * totals[i] for i in range(6)]
    centre = [centre[i] + time_step * motion[i] for i in range(3)]
    spin = motion[3:6]
    turned = []
    for i in range(3):
        j, k = (i + 1) % 3, (i + 2) % 3
        for c in range(3):
            cross = spin[j] * rotation[3 * k + c] - spin[k] * rotation[3 * j + c]
            turned.append(rotation[3 * i + c] + time_step * cross)
    return turned + centre + motion


def cross(left, right):
    return [
        left[1] * right[2] - left[2] * right[1],
        left[2] * right[0] - left[0] * right[2],
        left[0] * right[1] - left[1] * right[0],
    ]


def split(values):
    high = values.astype(bf16)
    return high, (values - high.astype(f32)).astype(bf16)


def other(axis, step):
    count = lax.axis_size(axis)
    return lax.rem(lax.axis_index(axis) + (step + count), count)


def place(step_x, step_y, step_z):
    return (other("gx", step_x), other("gy", step_y), other("gz", step_z))


def owner_index():
    return lax.axis_index("gx") * lax.axis_size("gz") + lax.axis_index("gz")


def owner_place(step):
    count_z = lax.axis_size("gz")
    owners = lax.axis_size("gx") * count_z
    owner = lax.rem(owner_index() + step, owners)
    return owner, (lax.div(owner, count_z), lax.axis_index("gy"), lax.rem(owner, count_z))


def greet(places):
    barrier = pltpu.get_barrier_semaphore()
    for device in places:
        pl.semaphore_signal(barrier, inc=1, device_id=device, device_id_type=MESH)
    pl.semaphore_wait(barrier, len(places))


def remote(source, target, send, receive, device):
    copy = pltpu.make_async_remote_copy(
        src_ref=source,
        dst_ref=target,
        send_sem=send,
        recv_sem=receive,
        device_id=device,
        device_id_type=MESH,
    )
    copy.start()
    return copy


def deal_kernel(
    owners,
    index_ref,
    name_ref,
    tiles_ref,
    small_ref,
    slots_ref,
    contacts_ref,
    all_ref,
    out_slots,
    out_contacts,
    send_sem,
    recv_sem,
):
    cap, contact_cap = slots_ref.shape[1], contacts_ref.shape[1]
    width = cap + contact_cap
    row = lax.broadcasted_iota(jnp.int32, tiles_ref.shape[1:], 0)
    me = owner_index()

    def fill(k, owner, slots, contacts):
        for r in range(width):
            at = owner * width + r
            tile = jnp.where(row == 7, name_ref[at], tiles_ref[index_ref[at]])
            if r < cap:
                slots[k, r] = tile
            else:
                contacts[k, r - cap] = tile

    greet([owner_place(k)[1] for k in range(1, owners)])
    copies = []
    for k in range(1, owners):
        owner, device = owner_place(k)
        fill(k, owner, out_slots, out_contacts)
        pairs = (
            (out_slots.at[k], slots_ref.at[me]),
            (out_contacts.at[k], contacts_ref.at[me]),
            (small_ref, all_ref.at[me]),
        )
        for i, (source, target) in enumerate(pairs):
            copies.append(remote(source, target, send_sem.at[i, k], recv_sem.at[i, k], device))
    fill(me, me, slots_ref, contacts_ref)
    all_ref[me] = small_ref[...]
    for copy in copies:
        copy.wait()


def deal(owners, cap, index, name, tiles, small):
    nodes = tiles.shape[2]
    contact_cap = index.shape[0] // owners - cap
    vmem = pl.BlockSpec(memory_space=pltpu.VMEM)
    smem = pl.BlockSpec(memory_space=pltpu.SMEM)
    slots = (owners, cap, 8, nodes)
    contacts = (owners, contact_cap, 8, nodes)
    return pl.pallas_call(
        functools.partial(deal_kernel, owners),
        out_shape=(
            jax.ShapeDtypeStruct(slots, f32),
            jax.ShapeDtypeStruct(contacts, f32),
            jax.ShapeDtypeStruct((owners,) + small.shape, f32),
        ),
        in_specs=[smem, smem, vmem, vmem],
        out_specs=(vmem, vmem, vmem),
        scratch_shapes=[
            pltpu.VMEM(slots, f32),
            pltpu.VMEM(contacts, f32),
            pltpu.SemaphoreType.DMA((3, owners)),
            pltpu.SemaphoreType.DMA((3, owners)),
        ],
        compiler_params=pltpu.CompilerParams(
            collective_id=0, has_side_effects=True, vmem_limit_bytes=40 * 1024 * 1024
        ),
    )(index, name, tiles, small)


def moving(axis, way):
    return [q for q in range(19) if lattice_dirs[q][axis] == way]


corners = [(1, 1), (-1, -1), (1, -1), (-1, 1)]


def corner_dir(way_x, way_y):
    return [q for q in range(19) if tuple(lattice_dirs[q]) == (way_x, way_y, 0)][0]


def exchange_kernel(
    owners,
    count_y,
    size_y,
    post_ref,
    solid_ref,
    loads_ref,
    state_ref,
    fluid_ref,
    next_ref,
    depth_ref,
    z_out,
    z_in,
    x_out,
    x_in,
    y_out,
    y_in,
    corner_out,
    corner_in,
    owner_in,
    owner_sum,
    slab_in,
    send_sem,
    recv_sem,
    owner_send,
    owner_recv,
    slab_send,
    slab_recv,
):
    directions, plane, size_z = post_ref.shape
    size_x = plane // size_y
    ways = (1, -1)
    me = owner_index()
    greet(
        [owner_place(k)[1] for k in range(1, owners)]
        + [place(0, k, 0) for k in range(1, count_y)]
        + [place(way_x, way_y, 0) for way_x, way_y in corners]
    )
    owner_copies = [
        remote(loads_ref, owner_in.at[k], owner_send.at[k], owner_recv.at[k], owner_place(k)[1])
        for k in range(1, owners)
    ]
    owner_in[0] = loads_ref[...]
    lane = lax.broadcasted_iota(jnp.int32, (plane, size_z), 1)
    z_copies = []
    for i, way in enumerate(ways):
        packed = jnp.zeros((plane, size_z), f32)
        for p, q in enumerate(moving(2, way)):
            shift = (p + 1) % size_z if way > 0 else p
            values = post_ref[q]
            if shift:
                values = pltpu.roll(values, shift, 1)
            packed = jnp.where(lane == p, values, packed)
        z_out[i] = packed
        z_copies.append(remote(z_out.at[i], z_in.at[i], send_sem.at[i], recv_sem.at[i], place(0, 0, way)))
    for copy in z_copies:
        copy.wait()
    slot_of = {}
    for i, way in enumerate(ways):
        packed = z_in[i]
        for p, q in enumerate(moving(2, way)):
            slot_of[q] = len(slot_of)
            edge = 0 if way > 0 else size_z - 1
            shift = (edge - p) % size_z
            face = pltpu.roll(packed, shift, 1) if shift else packed
            rolled = pltpu.roll(post_ref[q], way % size_z, 1)
            depth_ref[slot_of[q]] = jnp.where(lane == edge, face, rolled)

    def block(q, x):
        rows = pl.ds(x * size_y, size_y)
        return depth_ref[slot_of[q], rows] if q in slot_of else post_ref[q, rows]

    copies = []
    for i, way in enumerate(ways):
        for p, q in enumerate(moving(0, way)):
            x_out[i, p] = block(q, size_x - 1 if way > 0 else 0)
        copies.append(
            remote(x_out.at[i], x_in.at[i], send_sem.at[2 + i], recv_sem.at[2 + i], place(way, 0, 0))
        )
    for i, way in enumerate(ways):
        edge = size_y - 1 if way > 0 else 0
        for p, q in enumerate(moving(1, way)):
            for x in range(size_x):
                y_out[i, p, x : x + 1] = block(q, x)[edge : edge + 1]
        copies.append(
            remote(y_out.at[i], y_in.at[i], send_sem.at[4 + i], recv_sem.at[4 + i], place(0, way, 0))
        )
    for i, (way_x, way_y) in enumerate(corners):
        edge = size_y - 1 if way_y > 0 else 0
        values = block(corner_dir(way_x, way_y), size_x - 1 if way_x > 0 else 0)
        corner_out[i] = jnp.broadcast_to(values[edge : edge + 1], (8, size_z))
        copies.append(
            remote(
                corner_out.at[i],
                corner_in.at[i],
                send_sem.at[6 + i],
                recv_sem.at[6 + i],
                place(way_x, way_y, 0),
            )
        )

    for copy in owner_copies:
        copy.wait()
    added = owner_in[me]
    for j in range(1, owners):
        added = added + owner_in[lax.rem(me - j + owners, owners)]
    owner_sum[...] = added
    slab_copies = [
        remote(owner_sum, slab_in.at[k], slab_send.at[k], slab_recv.at[k], place(0, k, 0))
        for k in range(1, count_y)
    ]
    slab_in[0] = added

    for copy in copies:
        copy.wait()
    y_row = lax.broadcasted_iota(jnp.int32, (size_y, size_z), 0)

    def moved(q, x):
        way_x, way_y = int(lattice_dirs[q][0]), int(lattice_dirs[q][1])
        from_x = x - way_x
        outside = from_x < 0 or from_x >= size_x
        if outside:
            values = x_in[ways.index(way_x), moving(0, way_x).index(q)]
        else:
            values = block(q, from_x)
        if way_y:
            if outside:
                line = corner_in[corners.index((way_x, way_y))][0:1]
            else:
                line = y_in[ways.index(way_y), moving(1, way_y).index(q)][from_x : from_x + 1]
            edge = 0 if way_y > 0 else size_y - 1
            values = jnp.where(y_row == edge, line, pltpu.roll(values, way_y % size_y, 0))
        return values

    for x in range(size_x):
        rows = pl.ds(x * size_y, size_y)
        wall = solid_ref[rows] > 0
        fluid_ref[0, rows] = moved(0, x)
        for q in range(1, directions, 2):
            here, there = moved(q, x), moved(q + 1, x)
            fluid_ref[q, rows] = jnp.where(wall, there, here)
            fluid_ref[q + 1, rows] = jnp.where(wall, here, there)

    for copy in slab_copies:
        copy.wait()
    slab = lax.axis_index("gy")
    added = slab_in[slab]
    for j in range(1, count_y):
        added = added + slab_in[lax.rem(slab - j + count_y, count_y)]
    values = state_ref[...]
    after = advance_rows([values[i : i + 1] for i in range(18)], [added[i : i + 1] for i in range(6)])
    for i in range(18):
        next_ref[i : i + 1] = after[i]


def exchange(owners, count_y, size_y, post, solid, loads, state):
    directions, plane, size_z = post.shape
    size_x = plane // size_y
    vmem = pl.BlockSpec(memory_space=pltpu.VMEM)
    sides = len(moving(0, 1))
    dma = pltpu.SemaphoreType.DMA
    return pl.pallas_call(
        functools.partial(exchange_kernel, owners, count_y, size_y),
        out_shape=(jax.ShapeDtypeStruct(post.shape, f32), jax.ShapeDtypeStruct(state.shape, f32)),
        in_specs=[vmem] * 4,
        out_specs=(vmem, vmem),
        scratch_shapes=[
            pltpu.VMEM((2 * sides, plane, size_z), f32),
            pltpu.VMEM((2, plane, size_z), f32),
            pltpu.VMEM((2, plane, size_z), f32),
            pltpu.VMEM((2, sides, size_y, size_z), f32),
            pltpu.VMEM((2, sides, size_y, size_z), f32),
            pltpu.VMEM((2, sides, size_x, size_z), f32),
            pltpu.VMEM((2, sides, size_x, size_z), f32),
            pltpu.VMEM((4, 8, size_z), f32),
            pltpu.VMEM((4, 8, size_z), f32),
            pltpu.VMEM((owners,) + loads.shape, f32),
            pltpu.VMEM(loads.shape, f32),
            pltpu.VMEM((count_y,) + loads.shape, f32),
            dma((10,)),
            dma((10,)),
            dma((owners,)),
            dma((owners,)),
            dma((count_y,)),
            dma((count_y,)),
        ],
        compiler_params=pltpu.CompilerParams(
            collective_id=1, has_side_effects=True, vmem_limit_bytes=40 * 1024 * 1024
        ),
    )(post, solid, loads, state)


def columns(matrix, count):
    return [matrix[:, i : i + 1] for i in range(count)]


def lane_pack(values):
    rows = values[0].shape[0]
    lane = lax.broadcasted_iota(jnp.int32, (rows, 128), 1)
    out = jnp.zeros((rows, 128), f32)
    for i, value in enumerate(values):
        out = jnp.where(lane == i, value, out)
    return out


def total(values):
    return jnp.sum(values, axis=1, keepdims=True)


def step_kernel(
    size_y,
    tile_cap,
    chunk,
    counts_ref,
    pick_ref,
    state_ref,
    slots_ref,
    contacts_ref,
    holder_ref,
    coef_ref,
    fluid_ref,
    solid_ref,
    post_ref,
    loads_ref,
    poly_ref,
    level_ref,
    grid_ref,
    speed_ref,
    force_ref,
    cell_ref,
    velocity_ref,
):
    state = state_ref[...]
    grains = state.shape[1]
    tile_slots, _, nodes = slots_ref.shape
    contact_slots = contacts_ref.shape[0]
    order = coef_ref.shape[1]
    directions, plane, size_z = fluid_ref.shape
    size_x = plane // size_y

    def one_hot(ids):
        lane = lax.broadcasted_iota(jnp.int32, (ids.shape[0], grains), 1).astype(f32)
        return jnp.where(lane == ids, 1.0, 0.0)

    def picked(hot):
        found = lax.dot_general(
            hot, state, (((1,), (1,)), ((), ())), precision=highest, preferred_element_type=f32
        )
        return columns(found, 18)

    def gathered(values, hot):
        return lax.dot_general(
            lane_pack(values), hot, (((0,), (0,)), ((), ())), precision=highest, preferred_element_type=f32
        )[0:8]

    partner_hot = one_hot(contacts_ref[:, 7, :][:, 0:1])
    holder_hot = one_hot(holder_ref[...])
    partner = picked(partner_hot)
    holder = picked(holder_hot)
    alive = jnp.where(holder_ref[...] >= 0.0, 1.0, 0.0)
    body = [contacts_ref[:, i, :] for i in range(3)]
    arm = [
        partner[3 * i] * body[0] + partner[3 * i + 1] * body[1] + partner[3 * i + 2] * body[2]
        for i in range(3)
    ]
    rel = [(partner[9 + i] + arm[i]) - holder[9 + i] for i in range(3)]
    for d in range(3):
        y = jnp.clip(holder[d] * rel[0] + holder[3 + d] * rel[1] + holder[6 + d] * rel[2], -1.0, 1.0)
        first = [jnp.ones_like(y), y]
        second = [jnp.ones_like(y), 2.0 * y]
        for degree in range(2, order):
            first.append(2.0 * y * first[-1] - first[-2])
            second.append(2.0 * y * second[-1] - second[-2])
        for degree in range(order):
            slope = degree * second[degree - 1] if degree else jnp.zeros_like(y)
            poly_ref[2 * d, :, degree, :] = first[degree]
            poly_ref[2 * d + 1, :, degree, :] = slope

    def contact(slot, carry):
        high, low = split(coef_ref[pick_ref[slot]])
        table = jnp.concatenate([high, low, high], axis=0)
        along = jnp.concatenate([poly_ref[0, slot], poly_ref[1, slot]], axis=1)
        along_high, along_low = split(along)
        along = jnp.concatenate([along_high, along_high, along_low], axis=0)
        part = lax.dot_general(table, along, (((0,), (0,)), ((), ())), preferred_element_type=f32)
        poly_y, slope_y = poly_ref[2, slot], poly_ref[3, slot]
        poly_z, slope_z = poly_ref[4, slot], poly_ref[5, slot]
        value = slope_xp = slope_yp = None
        for b in range(order):
            here = part[b * order : (b + 1) * order, 0:nodes]
            there = part[b * order : (b + 1) * order, nodes : 2 * nodes]
            t, s = poly_y[b : b + 1], slope_y[b : b + 1]
            if b == 0:
                value, slope_xp, slope_yp = here * t, there * t, here * s
            else:
                value, slope_xp, slope_yp = value + here * t, slope_xp + there * t, slope_yp + here * s
        for i, terms in enumerate((value * poly_z, slope_xp * poly_z, slope_yp * poly_z, value * slope_z)):
            level_ref[i, pl.ds(slot, 1), :] = jnp.sum(terms, axis=0, keepdims=True)
        return carry

    lax.fori_loop(0, contact_slots, contact, 0, unroll=math.gcd(contact_slots, 4))

    gradient = [level_ref[i + 1] for i in range(3)]
    depth = jnp.maximum(-level_ref[0], 0.0)
    norm = gradient[0] * gradient[0] + gradient[1] * gradient[1] + gradient[2] * gradient[2]
    strength = contact_stiffness * depth / jnp.sqrt(1.0 + norm) * alive
    push = [
        (holder[3 * i] * gradient[0] + holder[3 * i + 1] * gradient[1] + holder[3 * i + 2] * gradient[2])
        * strength
        for i in range(3)
    ]
    sums = [total(push[i]) for i in range(3)]
    on_holder = [-s for s in sums] + [-total(t) for t in cross(rel, push)]
    on_partner = sums + [total(t) for t in cross(arm, push)]
    loads = gathered(on_holder, holder_hot) + gathered(on_partner, partner_hot)

    density = fluid_ref[0]
    momentum = [None, None, None]
    for q in range(1, directions):
        values = fluid_ref[q]
        density = density + values
        for i in range(3):
            e = int(lattice_dirs[q][i])
            if e:
                term = values if e > 0 else -values
                momentum[i] = term if momentum[i] is None else momentum[i] + term
    inverse = 1.0 / density
    for i in range(3):
        flow = momentum[i] * inverse
        velocity_ref[i] = flow
        high, low = split(flow)
        rows = pl.ds(i * plane, plane)
        grid_ref[rows, 0:size_z] = high
        grid_ref[rows, size_z : 2 * size_z] = low
        grid_ref[rows, 2 * size_z : 3 * size_z] = high

    slot_hot = one_hot(slots_ref[:, 7, :][:, 0:1])
    own = picked(slot_hot)
    body = [slots_ref[:, i, :] for i in range(3)]
    arm = [own[3 * i] * body[0] + own[3 * i + 1] * body[1] + own[3 * i + 2] * body[2] for i in range(3)]
    swirl = cross(own[15:18], arm)
    for i in range(3):
        speed_ref[:, i, :] = own[12 + i] + swirl[i]
    force_ref[...] = jnp.zeros_like(force_ref)
    cell_ref[...] = jnp.zeros_like(cell_ref)
    depth_row = lax.broadcasted_iota(jnp.int32, (size_z, nodes), 0).astype(f32)
    y_row = lax.broadcasted_iota(jnp.int32, (size_y, nodes), 0).astype(f32)

    def spread(start):
        highs, lows, plane_weights = [], [], []
        for k in range(chunk):
            tile = slots_ref[start + k]
            cell = tile[6:7]
            line = jnp.floor((cell + 0.5) * (1.0 / size_z))
            base_z = cell - line * size_z
            base_x = jnp.floor((line + 0.5) * (1.0 / size_y))
            base_y = line - base_x * size_y
            upper, lower = tile[5:6], 1.0 - tile[5:6]
            upper_high = upper.astype(bf16).astype(f32)
            lower_high = lower.astype(bf16).astype(f32)
            at_low, at_high = depth_row == base_z, depth_row == base_z + 1.0
            highs.append(
                jnp.where(at_low, lower_high, jnp.where(at_high, upper_high, 0.0)).astype(bf16)
            )
            lows.append(
                jnp.where(
                    at_low, lower - lower_high, jnp.where(at_high, upper - upper_high, 0.0)
                ).astype(bf16)
            )
            frac_y = tile[4:5]
            weight_y = jnp.where(
                y_row == base_y, 1.0 - frac_y, jnp.where(y_row == base_y + 1.0, frac_y, 0.0)
            )
            frac_x = tile[3:4]
            rows = []
            for x in range(size_x):
                weight_x = jnp.where(
                    base_x == float(x), 1.0 - frac_x, jnp.where(base_x == float(x - 1), frac_x, 0.0)
                )
                rows.append(weight_x * weight_y)
            plane_weights.append(jnp.concatenate(rows, axis=0))
        high = jnp.concatenate(highs, axis=1)
        low = jnp.concatenate(lows, axis=1)
        lines = jnp.dot(
            grid_ref[...], jnp.concatenate([high, high, low], axis=0), preferred_element_type=f32
        )
        spread_high, spread_low = [], []
        for k in range(chunk):
            weights = plane_weights[k]
            live = jnp.where(slots_ref[start + k][7:8] >= 0.0, ib_stiffness, 0.0)
            speed = speed_ref[start + k]
            pieces, forces = [], []
            for i in range(3):
                taken = lines[i * plane : (i + 1) * plane, k * nodes : (k + 1) * nodes]
                interp = jnp.sum(taken * weights, axis=0, keepdims=True)
                node = live * (speed[i : i + 1] - interp)
                force_ref[start + k, i : i + 1, :] = node
                pieces.append(node * weights)
            piece_high, piece_low = split(jnp.concatenate(pieces, axis=0))
            spread_high.append(piece_high)
            spread_low.append(piece_low)
        contract = (((1,), (1,)), ((), ()))
        wide = lax.dot_general(
            jnp.concatenate(spread_high, axis=1),
            jnp.concatenate([high, low], axis=0),
            contract,
            preferred_element_type=f32,
        )
        narrow = lax.dot_general(
            jnp.concatenate(spread_low, axis=1), high, contract, preferred_element_type=f32
        )
        cell_ref[...] += wide[:, 0:size_z] + wide[:, size_z : 2 * size_z] + narrow

    for source in range(tile_slots // tile_cap):

        def body_of(turn, carry, source=source):
            spread(source * tile_cap + turn * chunk)
            return carry

        lax.fori_loop(0, (counts_ref[source] + chunk - 1) // chunk, body_of, 0)

    node = [force_ref[:, i, :] for i in range(3)]
    back = [-total(node[i]) for i in range(3)] + [-total(t) for t in cross(arm, node)]
    loads_ref[...] = loads + gathered(back, slot_hot)

    for x in range(size_x):
        rows = slice(x * size_y, (x + 1) * size_y)
        density = fluid_ref[0, rows]
        for q in range(1, directions):
            density = density + fluid_ref[q, rows]
        scale = tau_relax / density
        shifted = [
            velocity_ref[i, rows] + scale * cell_ref[i * plane + x * size_y : i * plane + (x + 1) * size_y, :]
            for i in range(3)
        ]
        speed = shifted[0] * shifted[0] + shifted[1] * shifted[1] + shifted[2] * shifted[2]
        base = 1.0 - 1.5 * speed
        wall = solid_ref[rows] > 0
        for q in range(directions):
            flat = fluid_ref[q, rows]
            along = None
            for i in range(3):
                e = int(lattice_dirs[q][i])
                if e:
                    term = shifted[i] if e > 0 else -shifted[i]
                    along = term if along is None else along + term
            inside = base if along is None else base + along * (3.0 + 4.5 * along)
            balance = lattice_weights[q] * density * inside
            relaxed = flat - (flat - balance) * (1.0 / tau_relax)
            post_ref[q, rows] = jnp.where(wall, flat, relaxed)


def run_step(size_y, tile_cap, counts, pick, state, slots, contacts, holder, coefs, fluid, solid):
    grains = state.shape[1]
    tile_slots, _, nodes = slots.shape
    contact_slots = contacts.shape[0]
    order = coefs.shape[1]
    directions, plane, size_z = fluid.shape
    vmem = pl.BlockSpec(memory_space=pltpu.VMEM)
    smem = pl.BlockSpec(memory_space=pltpu.SMEM)
    return pl.pallas_call(
        functools.partial(step_kernel, size_y, tile_cap, math.gcd(tile_cap, 4)),
        out_shape=(
            jax.ShapeDtypeStruct(fluid.shape, f32),
            jax.ShapeDtypeStruct((8, grains), f32),
        ),
        in_specs=[smem, smem] + [vmem] * 7,
        out_specs=(vmem, vmem),
        scratch_shapes=[
            pltpu.VMEM((6, contact_slots, order, nodes), f32),
            pltpu.VMEM((4, contact_slots, nodes), f32),
            pltpu.VMEM((3 * plane, 3 * size_z), bf16),
            pltpu.VMEM((tile_slots, 8, nodes), f32),
            pltpu.VMEM((tile_slots, 8, nodes), f32),
            pltpu.VMEM((3 * plane, size_z), f32),
            pltpu.VMEM((3, plane, size_z), f32),
        ],
        compiler_params=pltpu.CompilerParams(vmem_limit_bytes=40 * 1024 * 1024),
    )(counts, pick, state, slots, contacts, holder, coefs, fluid, solid)


def per_device(
    populations,
    solid,
    coefficients,
    body_nodes,
    centers,
    angles,
    velocity,
    node_frac,
    node_cell,
    grain_tile,
    send_grain,
    recv_partner,
):
    directions, size_x, size_y, size_z = populations.shape
    plane = size_x * size_y
    grains = centers.shape[1]
    nodes = body_nodes.shape[1]
    count_z = lax.axis_size("gz")
    owners = lax.axis_size("gx") * count_z
    tile_cap = max(2, 2 * grains // owners)
    tile_slots = owners * tile_cap
    contact_slots = send_grain.shape[1]
    contact_cap = contact_slots // owners
    me = lax.axis_index("gx") * count_z + lax.axis_index("gz")
    first = (me * grains).astype(f32)

    route = grain_tile[0, :, 0]
    hot = (route[:, None] == jnp.arange(owners, dtype=jnp.int32)[None, :]).astype(jnp.int32)
    below = np.tril(np.ones((grains, grains), np.int32), -1)
    earlier = (route[:, None] == route[None, :]) & (below > 0)
    rank = jnp.sum(earlier.astype(jnp.int32), axis=1)
    slot_of = route * tile_cap + rank
    match = slot_of[:, None] == jnp.arange(tile_slots, dtype=jnp.int32)[None, :]
    grain_ids = jnp.arange(grains, dtype=jnp.int32)
    slot_grain = jnp.sum(jnp.where(match, grain_ids[:, None] + 1, 0), axis=0) - 1
    chosen = jnp.concatenate(
        [slot_grain.reshape(owners, tile_cap), send_grain[0].reshape(owners, contact_cap)], axis=1
    ).reshape(-1)
    name = jnp.where(chosen >= 0, chosen.astype(f32) + first, -1.0)
    tiles = jnp.concatenate(
        [body_nodes, node_frac, node_cell.astype(f32)[None], jnp.zeros((1, nodes, grains), f32)]
    ).transpose(2, 0, 1)
    rows = rotation_rows(angles) + [centers[i] for i in range(3)] + [velocity[i] for i in range(6)]
    small = jnp.pad(jnp.stack(rows), ((0, 6), (0, -grains % 128)))
    slots, contacts, everyone = deal(owners, tile_cap, jnp.maximum(chosen, 0), name, tiles, small)
    slots = slots.reshape(tile_slots, 8, nodes)
    contacts = contacts.reshape(contact_slots, 8, nodes)
    state = everyone[:, :18, :grains].transpose(1, 0, 2).reshape(18, owners * grains)
    counts = jnp.sum((slots[:, 7, 0].reshape(owners, tile_cap) >= 0.0).astype(jnp.int32), axis=1)
    recv = recv_partner[0]
    pick = jnp.maximum(recv, 0)
    holder = jnp.where(recv >= 0, recv.astype(f32) + first, -1.0)[:, None]

    solid_flat = solid.reshape(plane, size_z)
    fluid = populations.reshape(directions, plane, size_z)
    for step in range(STEPS):
        post, loads = run_step(
            size_y,
            tile_cap,
            counts,
            pick,
            state,
            slots,
            contacts,
            holder,
            coefficients,
            fluid,
            solid_flat,
        )
        fluid, state = exchange(owners, lax.axis_size("gy"), size_y, post, solid_flat, loads, state)
    state = lax.dynamic_slice_in_dim(state, me * grains, grains, axis=1)
    return (fluid.reshape(populations.shape), state[9:12], state[12:18])


def solution(mesh):
    in_specs = (
        P(None, "gx", "gy", "gz"),
        P("gx", "gy", "gz"),
        P(("gx", "gz"), None, None),
        P(None, "gy", ("gx", "gz")),
        P(None, ("gx", "gz")),
        P(None, ("gx", "gz")),
        P(None, ("gx", "gz")),
        P(None, "gy", ("gx", "gz")),
        P("gy", ("gx", "gz")),
        P("gy", ("gx", "gz"), None),
        P(("gx", "gz"), None),
        P(("gx", "gz"), None),
    )
    out_specs = (P(None, "gx", "gy", "gz"), P(None, ("gx", "gz")), P(None, ("gx", "gz")))
    return jax.shard_map(
        per_device, mesh=mesh, in_specs=in_specs, out_specs=out_specs, check_vma=False
    )
```

```python
import functools
import math

import jax
import jax.numpy as jnp
import numpy as np
from jax import lax
from jax.experimental import pallas as pl
from jax.experimental.pallas import tpu as pltpu
from jax.sharding import PartitionSpec as P

STEPS = 2

highest = lax.Precision.HIGHEST
lattice_dirs = np.array(
    [
        [0, 0, 0],
        [1, 0, 0],
        [-1, 0, 0],
        [0, 1, 0],
        [0, -1, 0],
        [0, 0, 1],
        [0, 0, -1],
        [1, 1, 0],
        [-1, -1, 0],
        [1, -1, 0],
        [-1, 1, 0],
        [1, 0, 1],
        [-1, 0, -1],
        [1, 0, -1],
        [-1, 0, 1],
        [0, 1, 1],
        [0, -1, -1],
        [0, 1, -1],
        [0, -1, 1],
    ],
    dtype=np.int32,
)
lattice_weights = [1.0 / 3.0] + [1.0 / 18.0] * 6 + [1.0 / 36.0] * 12
tau_relax = 0.9
ib_stiffness = 0.5
contact_stiffness = 0.05
time_step = 0.05
bf16 = jnp.bfloat16
f32 = jnp.float32
MESH = pl.DeviceIdType.MESH


def rotation_rows(cosine, sine):
    ca, cb, cc = cosine
    sa, sb, sc = sine
    return [
        cc * cb,
        cc * sb * sa - sc * ca,
        cc * sb * ca + sc * sa,
        sc * cb,
        sc * sb * sa + cc * ca,
        sc * sb * ca - cc * sa,
        -sb,
        cb * sa,
        cb * ca,
    ]


def advance_rows(rows, totals):
    rotation, centre, motion = rows[0:9], rows[9:12], rows[12:18]
    motion = [motion[i] + time_step * totals[i] for i in range(6)]
    centre = [centre[i] + time_step * motion[i] for i in range(3)]
    spin = motion[3:6]
    turned = []
    for i in range(3):
        j, k = (i + 1) % 3, (i + 2) % 3
        for c in range(3):
            cross = spin[j] * rotation[3 * k + c] - spin[k] * rotation[3 * j + c]
            turned.append(rotation[3 * i + c] + time_step * cross)
    return turned + centre + motion


def cross(left, right):
    return [
        left[1] * right[2] - left[2] * right[1],
        left[2] * right[0] - left[0] * right[2],
        left[0] * right[1] - left[1] * right[0],
    ]


def split(values):
    high = values.astype(bf16)
    return high, (values - high.astype(f32)).astype(bf16)


def other(axis, step):
    count = lax.axis_size(axis)
    return lax.rem(lax.axis_index(axis) + (step + count), count)


def place(step_x, step_y, step_z):
    return (other("gx", step_x), other("gy", step_y), other("gz", step_z))


def owner_index():
    return lax.axis_index("gx") * lax.axis_size("gz") + lax.axis_index("gz")


def owner_place(step):
    count_z = lax.axis_size("gz")
    owners = lax.axis_size("gx") * count_z
    owner = lax.rem(owner_index() + step, owners)
    return owner, (lax.div(owner, count_z), lax.axis_index("gy"), lax.rem(owner, count_z))


def greet(places):
    barrier = pltpu.get_barrier_semaphore()
    for device in places:
        pl.semaphore_signal(barrier, inc=1, device_id=device, device_id_type=MESH)
    pl.semaphore_wait(barrier, len(places))


def remote(source, target, send, receive, device):
    copy = pltpu.make_async_remote_copy(
        src_ref=source,
        dst_ref=target,
        send_sem=send,
        recv_sem=receive,
        device_id=device,
        device_id_type=MESH,
    )
    copy.start()
    return copy


def plan_kernel(
    route_ref,
    send_ref,
    tiles_ref,
    angles_ref,
    centers_ref,
    velocity_ref,
    slots_ref,
    contacts_ref,
    small_ref,
    count_ref,
):
    grains = tiles_ref.shape[0]
    row = lax.broadcasted_iota(jnp.int32, tiles_ref.shape[1:], 0)
    slots_ref[...] = jnp.full(slots_ref.shape, -1.0, f32)
    for owner in range(slots_ref.shape[0]):
        count_ref[owner] = 0

    def put(grain, carry):
        owner = route_ref[grain]
        rank = count_ref[owner]
        count_ref[owner] = rank + 1
        slots_ref[owner, rank] = jnp.where(row == 7, grain.astype(f32), tiles_ref[grain])
        return carry

    lax.fori_loop(0, grains, put, 0, unroll=8)

    def touch(slot, carry):
        grain = send_ref[slot]
        contacts_ref[slot] = jnp.where(row == 7, grain.astype(f32), tiles_ref[jnp.maximum(grain, 0)])
        return carry

    lax.fori_loop(0, contacts_ref.shape[0], touch, 0, unroll=8)
    angles = angles_ref[...]
    cosine, sine = jnp.cos(angles), jnp.sin(angles)
    small_ref[...] = jnp.zeros_like(small_ref)
    rows = rotation_rows([cosine[i : i + 1] for i in range(3)], [sine[i : i + 1] for i in range(3)])
    for i, values in enumerate(rows):
        small_ref[i : i + 1, 0:grains] = values
    small_ref[9:12, 0:grains] = centers_ref[...]
    small_ref[12:18, 0:grains] = velocity_ref[...]


def plan(owners, cap, route, send, tiles, angles, centers, velocity):
    grains, _, nodes = tiles.shape
    vmem = pl.BlockSpec(memory_space=pltpu.VMEM)
    smem = pl.BlockSpec(memory_space=pltpu.SMEM)
    return pl.pallas_call(
        plan_kernel,
        out_shape=(
            jax.ShapeDtypeStruct((owners, cap, 8, nodes), f32),
            jax.ShapeDtypeStruct((send.shape[0], 8, nodes), f32),
            jax.ShapeDtypeStruct((24, -(-grains // 128) * 128), f32),
        ),
        in_specs=[smem, smem] + [vmem] * 4,
        out_specs=(vmem, vmem, vmem),
        scratch_shapes=[pltpu.SMEM((owners,), jnp.int32)],
        compiler_params=pltpu.CompilerParams(vmem_limit_bytes=40 * 1024 * 1024),
    )(route, send, tiles, angles, centers, velocity)


def deal_kernel(
    owners,
    out_slots,
    out_contacts,
    small_ref,
    slots_ref,
    contacts_ref,
    all_ref,
    send_sem,
    recv_sem,
):
    me = owner_index()
    greet([owner_place(k)[1] for k in range(1, owners)])
    copies = []
    for k in range(1, owners):
        owner, device = owner_place(k)
        pairs = (
            (out_contacts.at[owner], contacts_ref.at[me]),
            (small_ref, all_ref.at[me]),
            (out_slots.at[owner], slots_ref.at[me]),
        )
        for i, (source, target) in enumerate(pairs):
            copies.append(remote(source, target, send_sem.at[i, k], recv_sem.at[i, k], device))
    slots_ref[me] = out_slots[me]
    contacts_ref[me] = out_contacts[me]
    all_ref[me] = small_ref[...]
    for copy in copies:
        copy.wait()


def deal(slots, contacts, small):
    owners = slots.shape[0]
    vmem = pl.BlockSpec(memory_space=pltpu.VMEM)
    return pl.pallas_call(
        functools.partial(deal_kernel, owners),
        out_shape=(
            jax.ShapeDtypeStruct(slots.shape, f32),
            jax.ShapeDtypeStruct(contacts.shape, f32),
            jax.ShapeDtypeStruct((owners,) + small.shape, f32),
        ),
        in_specs=[vmem, vmem, vmem],
        out_specs=(vmem, vmem, vmem),
        scratch_shapes=[
            pltpu.SemaphoreType.DMA((3, owners)),
            pltpu.SemaphoreType.DMA((3, owners)),
        ],
        compiler_params=pltpu.CompilerParams(
            collective_id=0, has_side_effects=True, vmem_limit_bytes=40 * 1024 * 1024
        ),
    )(slots, contacts, small)


def moving(axis, way):
    return [q for q in range(19) if lattice_dirs[q][axis] == way]


corners = [(1, 1), (-1, -1), (1, -1), (-1, 1)]


def corner_dir(way_x, way_y):
    return [q for q in range(19) if tuple(lattice_dirs[q]) == (way_x, way_y, 0)][0]


def exchange_kernel(
    owners,
    count_y,
    size_y,
    post_ref,
    solid_ref,
    loads_ref,
    state_ref,
    fluid_ref,
    next_ref,
    depth_ref,
    z_out,
    z_in,
    x_out,
    x_in,
    y_out,
    y_in,
    corner_out,
    corner_in,
    owner_in,
    owner_sum,
    slab_in,
    send_sem,
    recv_sem,
    owner_send,
    owner_recv,
    slab_send,
    slab_recv,
):
    directions, plane, size_z = post_ref.shape
    size_x = plane // size_y
    ways = (1, -1)
    me = owner_index()
    greet(
        [owner_place(k)[1] for k in range(1, owners)]
        + [place(0, k, 0) for k in range(1, count_y)]
        + [place(way_x, way_y, 0) for way_x, way_y in corners]
    )
    owner_copies = [
        remote(loads_ref, owner_in.at[k], owner_send.at[k], owner_recv.at[k], owner_place(k)[1])
        for k in range(1, owners)
    ]
    owner_in[0] = loads_ref[...]
    lane = lax.broadcasted_iota(jnp.int32, (plane, size_z), 1)
    z_copies = []
    for i, way in enumerate(ways):
        packed = jnp.zeros((plane, size_z), f32)
        for p, q in enumerate(moving(2, way)):
            shift = (p + 1) % size_z if way > 0 else p
            values = post_ref[q]
            if shift:
                values = pltpu.roll(values, shift, 1)
            packed = jnp.where(lane == p, values, packed)
        z_out[i] = packed
        z_copies.append(remote(z_out.at[i], z_in.at[i], send_sem.at[i], recv_sem.at[i], place(0, 0, way)))
    for copy in z_copies:
        copy.wait()
    slot_of = {}
    for i, way in enumerate(ways):
        packed = z_in[i]
        for p, q in enumerate(moving(2, way)):
            slot_of[q] = len(slot_of)
            edge = 0 if way > 0 else size_z - 1
            shift = (edge - p) % size_z
            face = pltpu.roll(packed, shift, 1) if shift else packed
            rolled = pltpu.roll(post_ref[q], way % size_z, 1)
            depth_ref[slot_of[q]] = jnp.where(lane == edge, face, rolled)

    def block(q, x):
        rows = pl.ds(x * size_y, size_y)
        return depth_ref[slot_of[q], rows] if q in slot_of else post_ref[q, rows]

    copies = []
    for i, way in enumerate(ways):
        for p, q in enumerate(moving(0, way)):
            x_out[i, p] = block(q, size_x - 1 if way > 0 else 0)
        copies.append(
            remote(x_out.at[i], x_in.at[i], send_sem.at[2 + i], recv_sem.at[2 + i], place(way, 0, 0))
        )
    for i, way in enumerate(ways):
        edge = size_y - 1 if way > 0 else 0
        for p, q in enumerate(moving(1, way)):
            for x in range(size_x):
                y_out[i, p, x : x + 1] = block(q, x)[edge : edge + 1]
        copies.append(
            remote(y_out.at[i], y_in.at[i], send_sem.at[4 + i], recv_sem.at[4 + i], place(0, way, 0))
        )
    for i, (way_x, way_y) in enumerate(corners):
        edge = size_y - 1 if way_y > 0 else 0
        values = block(corner_dir(way_x, way_y), size_x - 1 if way_x > 0 else 0)
        corner_out[i] = jnp.broadcast_to(values[edge : edge + 1], (8, size_z))
        copies.append(
            remote(
                corner_out.at[i],
                corner_in.at[i],
                send_sem.at[6 + i],
                recv_sem.at[6 + i],
                place(way_x, way_y, 0),
            )
        )

    for copy in owner_copies:
        copy.wait()
    added = owner_in[me]
    for j in range(1, owners):
        added = added + owner_in[lax.rem(me - j + owners, owners)]
    owner_sum[...] = added
    slab_copies = [
        remote(owner_sum, slab_in.at[k], slab_send.at[k], slab_recv.at[k], place(0, k, 0))
        for k in range(1, count_y)
    ]
    slab_in[0] = added

    for copy in copies:
        copy.wait()
    y_row = lax.broadcasted_iota(jnp.int32, (size_y, size_z), 0)

    def moved(q, x):
        way_x, way_y = int(lattice_dirs[q][0]), int(lattice_dirs[q][1])
        from_x = x - way_x
        outside = from_x < 0 or from_x >= size_x
        if outside:
            values = x_in[ways.index(way_x), moving(0, way_x).index(q)]
        else:
            values = block(q, from_x)
        if way_y:
            if outside:
                line = corner_in[corners.index((way_x, way_y))][0:1]
            else:
                line = y_in[ways.index(way_y), moving(1, way_y).index(q)][from_x : from_x + 1]
            edge = 0 if way_y > 0 else size_y - 1
            values = jnp.where(y_row == edge, line, pltpu.roll(values, way_y % size_y, 0))
        return values

    for x in range(size_x):
        rows = pl.ds(x * size_y, size_y)
        wall = solid_ref[rows] > 0
        fluid_ref[0, rows] = moved(0, x)
        for q in range(1, directions, 2):
            here, there = moved(q, x), moved(q + 1, x)
            fluid_ref[q, rows] = jnp.where(wall, there, here)
            fluid_ref[q + 1, rows] = jnp.where(wall, here, there)

    for copy in slab_copies:
        copy.wait()
    slab = lax.axis_index("gy")
    added = slab_in[slab]
    for j in range(1, count_y):
        added = added + slab_in[lax.rem(slab - j + count_y, count_y)]
    values = state_ref[...]
    after = advance_rows([values[i : i + 1] for i in range(18)], [added[i : i + 1] for i in range(6)])
    for i in range(18):
        next_ref[i : i + 1] = after[i]


def exchange(owners, count_y, size_y, post, solid, loads, state):
    directions, plane, size_z = post.shape
    size_x = plane // size_y
    vmem = pl.BlockSpec(memory_space=pltpu.VMEM)
    sides = len(moving(0, 1))
    dma = pltpu.SemaphoreType.DMA
    return pl.pallas_call(
        functools.partial(exchange_kernel, owners, count_y, size_y),
        out_shape=(jax.ShapeDtypeStruct(post.shape, f32), jax.ShapeDtypeStruct(state.shape, f32)),
        in_specs=[vmem] * 4,
        out_specs=(vmem, vmem),
        scratch_shapes=[
            pltpu.VMEM((2 * sides, plane, size_z), f32),
            pltpu.VMEM((2, plane, size_z), f32),
            pltpu.VMEM((2, plane, size_z), f32),
            pltpu.VMEM((2, sides, size_y, size_z), f32),
            pltpu.VMEM((2, sides, size_y, size_z), f32),
            pltpu.VMEM((2, sides, size_x, size_z), f32),
            pltpu.VMEM((2, sides, size_x, size_z), f32),
            pltpu.VMEM((4, 8, size_z), f32),
            pltpu.VMEM((4, 8, size_z), f32),
            pltpu.VMEM((owners,) + loads.shape, f32),
            pltpu.VMEM(loads.shape, f32),
            pltpu.VMEM((count_y,) + loads.shape, f32),
            dma((10,)),
            dma((10,)),
            dma((owners,)),
            dma((owners,)),
            dma((count_y,)),
            dma((count_y,)),
        ],
        compiler_params=pltpu.CompilerParams(
            collective_id=1, has_side_effects=True, vmem_limit_bytes=40 * 1024 * 1024
        ),
    )(post, solid, loads, state)


def columns(matrix, count):
    return [matrix[:, i : i + 1] for i in range(count)]


def lane_pack(values):
    rows = values[0].shape[0]
    lane = lax.broadcasted_iota(jnp.int32, (rows, 128), 1)
    out = jnp.zeros((rows, 128), f32)
    for i, value in enumerate(values):
        out = jnp.where(lane == i, value, out)
    return out


def total(values):
    return jnp.sum(values, axis=1, keepdims=True)


def step_kernel(
    size_y,
    tile_cap,
    owned,
    chunk,
    group,
    pick_ref,
    state_ref,
    slots_ref,
    contacts_ref,
    holder_ref,
    coef_ref,
    fluid_ref,
    solid_ref,
    post_ref,
    loads_ref,
    poly_ref,
    level_ref,
    grid_ref,
    speed_ref,
    force_ref,
    cell_ref,
    velocity_ref,
):
    state = state_ref[...]
    grains = state.shape[1]
    tile_slots, _, nodes = slots_ref.shape
    contact_slots = contacts_ref.shape[0]
    order = coef_ref.shape[1]
    directions, plane, size_z = fluid_ref.shape
    size_x = plane // size_y

    def one_hot(ids):
        lane = lax.broadcasted_iota(jnp.int32, (ids.shape[0], grains), 1).astype(f32)
        return jnp.where(lane == ids, 1.0, 0.0)

    def named(tiles_ref, per_source):
        ids = tiles_ref[:, 7, :][:, 0:1]
        source = lax.broadcasted_iota(jnp.int32, ids.shape, 0).astype(f32)
        source = jnp.floor((source + 0.5) * (1.0 / per_source))
        return jnp.where(ids >= 0.0, ids + source * owned, -1.0)

    def picked(hot):
        found = lax.dot_general(
            hot, state, (((1,), (1,)), ((), ())), precision=highest, preferred_element_type=f32
        )
        return columns(found, 18)

    def gathered(values, hot):
        return lax.dot_general(
            lane_pack(values), hot, (((0,), (0,)), ((), ())), precision=highest, preferred_element_type=f32
        )[0:8]

    partner_hot = one_hot(named(contacts_ref, contact_slots // (tile_slots // tile_cap)))
    holder_hot = one_hot(holder_ref[...])
    partner = picked(partner_hot)
    holder = picked(holder_hot)
    alive = jnp.where(holder_ref[...] >= 0.0, 1.0, 0.0)
    body = [contacts_ref[:, i, :] for i in range(3)]
    arm = [
        partner[3 * i] * body[0] + partner[3 * i + 1] * body[1] + partner[3 * i + 2] * body[2]
        for i in range(3)
    ]
    rel = [(partner[9 + i] + arm[i]) - holder[9 + i] for i in range(3)]
    for d in range(3):
        y = jnp.clip(holder[d] * rel[0] + holder[3 + d] * rel[1] + holder[6 + d] * rel[2], -1.0, 1.0)
        first = [jnp.ones_like(y), y]
        second = [jnp.ones_like(y), 2.0 * y]
        for degree in range(2, order):
            first.append(2.0 * y * first[-1] - first[-2])
            second.append(2.0 * y * second[-1] - second[-2])
        for degree in range(order):
            slope = degree * second[degree - 1] if degree else jnp.zeros_like(y)
            poly_ref[2 * d, :, degree, :] = first[degree]
            poly_ref[2 * d + 1, :, degree, :] = slope

    def contact(slot, carry):
        high, low = split(coef_ref[pick_ref[slot]])
        table = jnp.concatenate([high, low, high], axis=0)
        along = jnp.concatenate([poly_ref[0, slot], poly_ref[1, slot]], axis=1)
        along_high, along_low = split(along)
        along = jnp.concatenate([along_high, along_high, along_low], axis=0)
        part = lax.dot_general(table, along, (((0,), (0,)), ((), ())), preferred_element_type=f32)
        poly_y, slope_y = poly_ref[2, slot], poly_ref[3, slot]
        poly_z, slope_z = poly_ref[4, slot], poly_ref[5, slot]
        value = slope_xp = slope_yp = None
        for b in range(order):
            here = part[b * order : (b + 1) * order, 0:nodes]
            there = part[b * order : (b + 1) * order, nodes : 2 * nodes]
            t, s = poly_y[b : b + 1], slope_y[b : b + 1]
            if b == 0:
                value, slope_xp, slope_yp = here * t, there * t, here * s
            else:
                value, slope_xp, slope_yp = value + here * t, slope_xp + there * t, slope_yp + here * s
        for i, terms in enumerate((value * poly_z, slope_xp * poly_z, slope_yp * poly_z, value * slope_z)):
            level_ref[i, pl.ds(slot, 1), :] = jnp.sum(terms, axis=0, keepdims=True)
        return carry

    lax.fori_loop(0, contact_slots, contact, 0, unroll=math.gcd(contact_slots, 4))

    gradient = [level_ref[i + 1] for i in range(3)]
    depth = jnp.maximum(-level_ref[0], 0.0)
    norm = gradient[0] * gradient[0] + gradient[1] * gradient[1] + gradient[2] * gradient[2]
    strength = contact_stiffness * depth / jnp.sqrt(1.0 + norm) * alive
    push = [
        (holder[3 * i] * gradient[0] + holder[3 * i + 1] * gradient[1] + holder[3 * i + 2] * gradient[2])
        * strength
        for i in range(3)
    ]
    sums = [total(push[i]) for i in range(3)]
    on_holder = [-s for s in sums] + [-total(t) for t in cross(rel, push)]
    on_partner = sums + [total(t) for t in cross(arm, push)]
    loads = gathered(on_holder, holder_hot) + gathered(on_partner, partner_hot)

    density = fluid_ref[0]
    momentum = [None, None, None]
    for q in range(1, directions):
        values = fluid_ref[q]
        density = density + values
        for i in range(3):
            e = int(lattice_dirs[q][i])
            if e:
                term = values if e > 0 else -values
                momentum[i] = term if momentum[i] is None else momentum[i] + term
    inverse = 1.0 / density
    for i in range(3):
        flow = momentum[i] * inverse
        velocity_ref[i] = flow
        high, low = split(flow)
        rows = pl.ds(i * plane, plane)
        grid_ref[rows, 0:size_z] = high
        grid_ref[rows, size_z : 2 * size_z] = low
        grid_ref[rows, 2 * size_z : 3 * size_z] = high

    slot_hot = one_hot(named(slots_ref, tile_cap))
    own = picked(slot_hot)
    body = [slots_ref[:, i, :] for i in range(3)]
    arm = [own[3 * i] * body[0] + own[3 * i + 1] * body[1] + own[3 * i + 2] * body[2] for i in range(3)]
    swirl = cross(own[15:18], arm)
    for i in range(3):
        speed_ref[:, i, :] = own[12 + i] + swirl[i]
    force_ref[...] = jnp.zeros_like(force_ref)
    cell_ref[...] = jnp.zeros_like(cell_ref)
    kind = bf16 if size_z <= 256 else f32
    depth_row = lax.broadcasted_iota(jnp.int32, (size_z, nodes), 0).astype(f32).astype(kind)
    y_row = lax.broadcasted_iota(jnp.int32, (size_y, nodes), 0).astype(f32)

    def weights_of(slot):
        tile = slots_ref[slot]
        cell = tile[6:7]
        line = jnp.floor((cell + 0.5) * (1.0 / size_z))
        base_z = cell - line * size_z
        base_x = jnp.floor((line + 0.5) * (1.0 / size_y))
        base_y = line - base_x * size_y
        upper, lower = tile[5:6], 1.0 - tile[5:6]
        upper_high, upper_low = split(upper)
        lower_high, lower_low = split(lower)
        none = jnp.zeros((size_z, nodes), kind)
        at_low, at_high = depth_row == base_z.astype(kind), depth_row == (base_z + 1.0).astype(kind)

        def placed(low_value, high_value):
            far = jnp.where(at_high, high_value.astype(kind), none)
            return jnp.where(at_low, low_value.astype(kind), far).astype(bf16)

        frac_y = tile[4:5]
        weight_y = jnp.where(
            y_row == base_y, 1.0 - frac_y, jnp.where(y_row == base_y + 1.0, frac_y, 0.0)
        )
        frac_x = tile[3:4]
        rows = []
        for x in range(size_x):
            weight_x = jnp.where(
                base_x == float(x), 1.0 - frac_x, jnp.where(base_x == float(x - 1), frac_x, 0.0)
            )
            rows.append(weight_x * weight_y)
        high, low = placed(lower_high, upper_high), placed(lower_low, upper_low)
        return high, low, jnp.concatenate(rows, axis=0)

    def spread(start):
        starts = [start + part * group for part in range(chunk // group)]
        sets = [[weights_of(first + k) for k in range(group)] for first in starts]
        highs = [jnp.concatenate([w[0] for w in each], axis=1) for each in sets]
        lows = [jnp.concatenate([w[1] for w in each], axis=1) for each in sets]
        lines = [
            jnp.dot(
                grid_ref[...], jnp.concatenate([high, high, low], axis=0), preferred_element_type=f32
            )
            for high, low in zip(highs, lows)
        ]
        added = None
        contract = (((1,), (1,)), ((), ()))
        for first, each, high, low, line in zip(starts, sets, highs, lows, lines):
            spread_high, spread_low = [], []
            for k in range(group):
                weights = each[k][2]
                live = jnp.where(slots_ref[first + k][7:8] >= 0.0, ib_stiffness, 0.0)
                speed = speed_ref[first + k]
                pieces = []
                for i in range(3):
                    taken = line[i * plane : (i + 1) * plane, k * nodes : (k + 1) * nodes]
                    interp = jnp.sum(taken * weights, axis=0, keepdims=True)
                    node = live * (speed[i : i + 1] - interp)
                    force_ref[first + k, i : i + 1, :] = node
                    pieces.append(node * weights)
                piece_high, piece_low = split(jnp.concatenate(pieces, axis=0))
                spread_high.append(piece_high)
                spread_low.append(piece_low)
            wide = lax.dot_general(
                jnp.concatenate(spread_high, axis=1),
                jnp.concatenate([high, low], axis=0),
                contract,
                preferred_element_type=f32,
            )
            narrow = lax.dot_general(
                jnp.concatenate(spread_low, axis=1), high, contract, preferred_element_type=f32
            )
            term = wide[:, 0:size_z] + wide[:, size_z : 2 * size_z] + narrow
            added = term if added is None else added + term
        cell_ref[...] += added

    for source in range(tile_slots // tile_cap):

        def body_of(turn, carry, source=source):
            spread(source * tile_cap + turn * chunk)
            return carry

        ids = slots_ref[source * tile_cap : (source + 1) * tile_cap, 7, :][:, 0:1]
        count = jnp.sum(jnp.where(ids >= 0.0, 1.0, 0.0)).astype(jnp.int32)
        lax.fori_loop(0, lax.div(count + (chunk - 1), chunk), body_of, 0)

    node = [force_ref[:, i, :] for i in range(3)]
    back = [-total(node[i]) for i in range(3)] + [-total(t) for t in cross(arm, node)]
    loads_ref[...] = loads + gathered(back, slot_hot)

    for x in range(size_x):
        rows = slice(x * size_y, (x + 1) * size_y)
        density = fluid_ref[0, rows]
        for q in range(1, directions):
            density = density + fluid_ref[q, rows]
        scale = tau_relax / density
        shifted = [
            velocity_ref[i, rows] + scale * cell_ref[i * plane + x * size_y : i * plane + (x + 1) * size_y, :]
            for i in range(3)
        ]
        speed = shifted[0] * shifted[0] + shifted[1] * shifted[1] + shifted[2] * shifted[2]
        base = 1.0 - 1.5 * speed
        wall = solid_ref[rows] > 0
        for q in range(directions):
            flat = fluid_ref[q, rows]
            along = None
            for i in range(3):
                e = int(lattice_dirs[q][i])
                if e:
                    term = shifted[i] if e > 0 else -shifted[i]
                    along = term if along is None else along + term
            inside = base if along is None else base + along * (3.0 + 4.5 * along)
            balance = lattice_weights[q] * density * inside
            relaxed = flat - (flat - balance) * (1.0 / tau_relax)
            post_ref[q, rows] = jnp.where(wall, flat, relaxed)


def run_step(size_y, tile_cap, owned, pick, state, slots, contacts, holder, coefs, fluid, solid):
    grains = state.shape[1]
    tile_slots, _, nodes = slots.shape
    contact_slots = contacts.shape[0]
    order = coefs.shape[1]
    directions, plane, size_z = fluid.shape
    vmem = pl.BlockSpec(memory_space=pltpu.VMEM)
    smem = pl.BlockSpec(memory_space=pltpu.SMEM)
    return pl.pallas_call(
        functools.partial(
            step_kernel, size_y, tile_cap, owned, math.gcd(tile_cap, 8), math.gcd(tile_cap, 4)
        ),
        out_shape=(
            jax.ShapeDtypeStruct(fluid.shape, f32),
            jax.ShapeDtypeStruct((8, grains), f32),
        ),
        in_specs=[smem] + [vmem] * 7,
        out_specs=(vmem, vmem),
        scratch_shapes=[
            pltpu.VMEM((6, contact_slots, order, nodes), f32),
            pltpu.VMEM((4, contact_slots, nodes), f32),
            pltpu.VMEM((3 * plane, 3 * size_z), bf16),
            pltpu.VMEM((tile_slots, 8, nodes), f32),
            pltpu.VMEM((tile_slots, 8, nodes), f32),
            pltpu.VMEM((3 * plane, size_z), f32),
            pltpu.VMEM((3, plane, size_z), f32),
        ],
        compiler_params=pltpu.CompilerParams(vmem_limit_bytes=40 * 1024 * 1024),
    )(pick, state, slots, contacts, holder, coefs, fluid, solid)


def per_device(
    populations,
    solid,
    coefficients,
    body_nodes,
    centers,
    angles,
    velocity,
    node_frac,
    node_cell,
    grain_tile,
    send_grain,
    recv_partner,
):
    directions, size_x, size_y, size_z = populations.shape
    plane = size_x * size_y
    grains = centers.shape[1]
    nodes = body_nodes.shape[1]
    count_z = lax.axis_size("gz")
    owners = lax.axis_size("gx") * count_z
    tile_cap = max(2, 2 * grains // owners)
    tile_slots = owners * tile_cap
    contact_slots = send_grain.shape[1]
    contact_cap = contact_slots // owners
    me = lax.axis_index("gx") * count_z + lax.axis_index("gz")
    first = (me * grains).astype(f32)

    tiles = jnp.concatenate(
        [body_nodes, node_frac, node_cell.astype(f32)[None], jnp.zeros((1, nodes, grains), f32)]
    ).transpose(2, 0, 1)
    slots, contacts, small = plan(
        owners, tile_cap, grain_tile[0, :, 0], send_grain[0], tiles, angles, centers, velocity
    )
    slots, contacts, everyone = deal(slots, contacts.reshape(owners, contact_cap, 8, nodes), small)
    slots = slots.reshape(tile_slots, 8, nodes)
    contacts = contacts.reshape(contact_slots, 8, nodes)
    state = everyone[:, :18, :grains].transpose(1, 0, 2).reshape(18, owners * grains)
    recv = recv_partner[0]
    pick = jnp.maximum(recv, 0)
    holder = jnp.where(recv >= 0, recv.astype(f32) + first, -1.0)[:, None]

    solid_flat = solid.reshape(plane, size_z)
    fluid = populations.reshape(directions, plane, size_z)
    for step in range(STEPS):
        post, loads = run_step(
            size_y,
            tile_cap,
            grains,
            pick,
            state,
            slots,
            contacts,
            holder,
            coefficients,
            fluid,
            solid_flat,
        )
        fluid, state = exchange(owners, lax.axis_size("gy"), size_y, post, solid_flat, loads, state)
    state = lax.dynamic_slice_in_dim(state, me * grains, grains, axis=1)
    return (fluid.reshape(populations.shape), state[9:12], state[12:18])


def solution(mesh):
    in_specs = (
        P(None, "gx", "gy", "gz"),
        P("gx", "gy", "gz"),
        P(("gx", "gz"), None, None),
        P(None, "gy", ("gx", "gz")),
        P(None, ("gx", "gz")),
        P(None, ("gx", "gz")),
        P(None, ("gx", "gz")),
        P(None, "gy", ("gx", "gz")),
        P("gy", ("gx", "gz")),
        P("gy", ("gx", "gz"), None),
        P(("gx", "gz"), None),
        P(("gx", "gz"), None),
    )
    out_specs = (P(None, "gx", "gy", "gz"), P(None, ("gx", "gz")), P(None, ("gx", "gz")))
    return jax.shard_map(
        per_device, mesh=mesh, in_specs=in_specs, out_specs=out_specs, check_vma=False
    )
```

```python
import functools
import math

import jax
import jax.numpy as jnp
import numpy as np
from jax import lax
from jax.experimental import pallas as pl
from jax.experimental.pallas import tpu as pltpu
from jax.sharding import PartitionSpec as P

STEPS = 2

highest = lax.Precision.HIGHEST
lattice_dirs = np.array(
    [
        [0, 0, 0],
        [1, 0, 0],
        [-1, 0, 0],
        [0, 1, 0],
        [0, -1, 0],
        [0, 0, 1],
        [0, 0, -1],
        [1, 1, 0],
        [-1, -1, 0],
        [1, -1, 0],
        [-1, 1, 0],
        [1, 0, 1],
        [-1, 0, -1],
        [1, 0, -1],
        [-1, 0, 1],
        [0, 1, 1],
        [0, -1, -1],
        [0, 1, -1],
        [0, -1, 1],
    ],
    dtype=np.int32,
)
lattice_weights = [1.0 / 3.0] + [1.0 / 18.0] * 6 + [1.0 / 36.0] * 12
tau_relax = 0.9
ib_stiffness = 0.5
contact_stiffness = 0.05
time_step = 0.05
bf16 = jnp.bfloat16
f32 = jnp.float32
MESH = pl.DeviceIdType.MESH


def rotation_rows(cosine, sine):
    ca, cb, cc = cosine
    sa, sb, sc = sine
    return [
        cc * cb,
        cc * sb * sa - sc * ca,
        cc * sb * ca + sc * sa,
        sc * cb,
        sc * sb * sa + cc * ca,
        sc * sb * ca - cc * sa,
        -sb,
        cb * sa,
        cb * ca,
    ]


def advance_rows(rows, totals):
    rotation, centre, motion = rows[0:9], rows[9:12], rows[12:18]
    motion = [motion[i] + time_step * totals[i] for i in range(6)]
    centre = [centre[i] + time_step * motion[i] for i in range(3)]
    spin = motion[3:6]
    turned = []
    for i in range(3):
        j, k = (i + 1) % 3, (i + 2) % 3
        for c in range(3):
            cross = spin[j] * rotation[3 * k + c] - spin[k] * rotation[3 * j + c]
            turned.append(rotation[3 * i + c] + time_step * cross)
    return turned + centre + motion


def cross(left, right):
    return [
        left[1] * right[2] - left[2] * right[1],
        left[2] * right[0] - left[0] * right[2],
        left[0] * right[1] - left[1] * right[0],
    ]


def split(values):
    high = values.astype(bf16)
    return high, (values - high.astype(f32)).astype(bf16)


def other(axis, step):
    count = lax.axis_size(axis)
    return lax.rem(lax.axis_index(axis) + (step + count), count)


def place(step_x, step_y, step_z):
    return (other("gx", step_x), other("gy", step_y), other("gz", step_z))


def owner_index():
    return lax.axis_index("gx") * lax.axis_size("gz") + lax.axis_index("gz")


def owner_place(step):
    count_z = lax.axis_size("gz")
    owners = lax.axis_size("gx") * count_z
    owner = lax.rem(owner_index() + step, owners)
    return owner, (lax.div(owner, count_z), lax.axis_index("gy"), lax.rem(owner, count_z))


def greet(places):
    barrier = pltpu.get_barrier_semaphore()
    for device in places:
        pl.semaphore_signal(barrier, inc=1, device_id=device, device_id_type=MESH)
    pl.semaphore_wait(barrier, len(places))


def remote(source, target, send, receive, device):
    copy = pltpu.make_async_remote_copy(
        src_ref=source,
        dst_ref=target,
        send_sem=send,
        recv_sem=receive,
        device_id=device,
        device_id_type=MESH,
    )
    copy.start()
    return copy


def plan_kernel(
    route_ref,
    send_ref,
    tiles_ref,
    angles_ref,
    centers_ref,
    velocity_ref,
    slots_ref,
    contacts_ref,
    small_ref,
    count_ref,
):
    grains = tiles_ref.shape[0]
    row = lax.broadcasted_iota(jnp.int32, tiles_ref.shape[1:], 0)
    slots_ref[...] = jnp.full(slots_ref.shape, -1.0, f32)
    for owner in range(slots_ref.shape[0]):
        count_ref[owner] = 0

    def put(grain, carry):
        owner = route_ref[grain]
        rank = count_ref[owner]
        count_ref[owner] = rank + 1
        slots_ref[owner, rank] = jnp.where(row == 7, grain.astype(f32), tiles_ref[grain])
        return carry

    lax.fori_loop(0, grains, put, 0, unroll=8)

    def touch(slot, carry):
        grain = send_ref[slot]
        contacts_ref[slot] = jnp.where(row == 7, grain.astype(f32), tiles_ref[jnp.maximum(grain, 0)])
        return carry

    lax.fori_loop(0, contacts_ref.shape[0], touch, 0, unroll=8)
    angles = angles_ref[...]
    cosine, sine = jnp.cos(angles), jnp.sin(angles)
    small_ref[...] = jnp.zeros_like(small_ref)
    rows = rotation_rows([cosine[i : i + 1] for i in range(3)], [sine[i : i + 1] for i in range(3)])
    for i, values in enumerate(rows):
        small_ref[i : i + 1, 0:grains] = values
    small_ref[9:12, 0:grains] = centers_ref[...]
    small_ref[12:18, 0:grains] = velocity_ref[...]


def plan(owners, cap, route, send, tiles, angles, centers, velocity):
    grains, _, nodes = tiles.shape
    vmem = pl.BlockSpec(memory_space=pltpu.VMEM)
    smem = pl.BlockSpec(memory_space=pltpu.SMEM)
    return pl.pallas_call(
        plan_kernel,
        out_shape=(
            jax.ShapeDtypeStruct((owners, cap, 8, nodes), f32),
            jax.ShapeDtypeStruct((send.shape[0], 8, nodes), f32),
            jax.ShapeDtypeStruct((24, -(-grains // 128) * 128), f32),
        ),
        in_specs=[smem, smem] + [vmem] * 4,
        out_specs=(vmem, vmem, vmem),
        scratch_shapes=[pltpu.SMEM((owners,), jnp.int32)],
        compiler_params=pltpu.CompilerParams(vmem_limit_bytes=40 * 1024 * 1024),
    )(route, send, tiles, angles, centers, velocity)


def deal_kernel(
    owners,
    out_slots,
    out_contacts,
    small_ref,
    slots_ref,
    contacts_ref,
    all_ref,
    send_sem,
    recv_sem,
):
    me = owner_index()
    greet([owner_place(k)[1] for k in range(1, owners)])
    copies = []
    for k in range(1, owners):
        owner, device = owner_place(k)
        pairs = (
            (out_contacts.at[owner], contacts_ref.at[me]),
            (small_ref, all_ref.at[me]),
            (out_slots.at[owner], slots_ref.at[me]),
        )
        for i, (source, target) in enumerate(pairs):
            copies.append(remote(source, target, send_sem.at[i, k], recv_sem.at[i, k], device))
    slots_ref[me] = out_slots[me]
    contacts_ref[me] = out_contacts[me]
    all_ref[me] = small_ref[...]
    for copy in copies:
        copy.wait()


def deal(slots, contacts, small):
    owners = slots.shape[0]
    vmem = pl.BlockSpec(memory_space=pltpu.VMEM)
    return pl.pallas_call(
        functools.partial(deal_kernel, owners),
        out_shape=(
            jax.ShapeDtypeStruct(slots.shape, f32),
            jax.ShapeDtypeStruct(contacts.shape, f32),
            jax.ShapeDtypeStruct((owners,) + small.shape, f32),
        ),
        in_specs=[vmem, vmem, vmem],
        out_specs=(vmem, vmem, vmem),
        scratch_shapes=[
            pltpu.SemaphoreType.DMA((3, owners)),
            pltpu.SemaphoreType.DMA((3, owners)),
        ],
        compiler_params=pltpu.CompilerParams(
            collective_id=0, has_side_effects=True, vmem_limit_bytes=40 * 1024 * 1024
        ),
    )(slots, contacts, small)


def moving(axis, way):
    return [q for q in range(19) if lattice_dirs[q][axis] == way]


corners = [(1, 1), (-1, -1), (1, -1), (-1, 1)]


def corner_dir(way_x, way_y):
    return [q for q in range(19) if tuple(lattice_dirs[q]) == (way_x, way_y, 0)][0]


def exchange_kernel(
    owners,
    count_y,
    size_y,
    post_ref,
    solid_ref,
    loads_ref,
    state_ref,
    fluid_ref,
    next_ref,
    depth_ref,
    z_out,
    z_in,
    x_out,
    x_in,
    y_out,
    y_in,
    corner_out,
    corner_in,
    owner_in,
    owner_sum,
    slab_in,
    send_sem,
    recv_sem,
    owner_send,
    owner_recv,
    slab_send,
    slab_recv,
):
    directions, plane, size_z = post_ref.shape
    size_x = plane // size_y
    ways = (1, -1)
    me = owner_index()
    greet(
        [owner_place(k)[1] for k in range(1, owners)]
        + [place(0, k, 0) for k in range(1, count_y)]
        + [place(way_x, way_y, 0) for way_x, way_y in corners]
    )
    owner_copies = [
        remote(loads_ref, owner_in.at[k], owner_send.at[k], owner_recv.at[k], owner_place(k)[1])
        for k in range(1, owners)
    ]
    owner_in[0] = loads_ref[...]
    lane = lax.broadcasted_iota(jnp.int32, (plane, size_z), 1)
    z_copies = []
    for i, way in enumerate(ways):
        packed = jnp.zeros((plane, size_z), f32)
        for p, q in enumerate(moving(2, way)):
            shift = (p + 1) % size_z if way > 0 else p
            values = post_ref[q]
            if shift:
                values = pltpu.roll(values, shift, 1)
            packed = jnp.where(lane == p, values, packed)
        z_out[i] = packed
        z_copies.append(remote(z_out.at[i], z_in.at[i], send_sem.at[i], recv_sem.at[i], place(0, 0, way)))
    for copy in z_copies:
        copy.wait()
    for copy in owner_copies:
        copy.wait()
    added = owner_in[me]
    for j in range(1, owners):
        added = added + owner_in[lax.rem(me - j + owners, owners)]
    owner_sum[...] = added
    slab_copies = [
        remote(owner_sum, slab_in.at[k], slab_send.at[k], slab_recv.at[k], place(0, k, 0))
        for k in range(1, count_y)
    ]
    slab_in[0] = added

    slot_of = {}
    for i, way in enumerate(ways):
        packed = z_in[i]
        for p, q in enumerate(moving(2, way)):
            slot_of[q] = len(slot_of)
            edge = 0 if way > 0 else size_z - 1
            shift = (edge - p) % size_z
            face = pltpu.roll(packed, shift, 1) if shift else packed
            rolled = pltpu.roll(post_ref[q], way % size_z, 1)
            depth_ref[slot_of[q]] = jnp.where(lane == edge, face, rolled)

    def block(q, x):
        rows = pl.ds(x * size_y, size_y)
        return depth_ref[slot_of[q], rows] if q in slot_of else post_ref[q, rows]

    copies = []
    for i, way in enumerate(ways):
        for p, q in enumerate(moving(0, way)):
            x_out[i, p] = block(q, size_x - 1 if way > 0 else 0)
        copies.append(
            remote(x_out.at[i], x_in.at[i], send_sem.at[2 + i], recv_sem.at[2 + i], place(way, 0, 0))
        )
    for i, way in enumerate(ways):
        edge = size_y - 1 if way > 0 else 0
        for p, q in enumerate(moving(1, way)):
            for x in range(size_x):
                y_out[i, p, x : x + 1] = block(q, x)[edge : edge + 1]
        copies.append(
            remote(y_out.at[i], y_in.at[i], send_sem.at[4 + i], recv_sem.at[4 + i], place(0, way, 0))
        )
    for i, (way_x, way_y) in enumerate(corners):
        edge = size_y - 1 if way_y > 0 else 0
        values = block(corner_dir(way_x, way_y), size_x - 1 if way_x > 0 else 0)
        corner_out[i] = jnp.broadcast_to(values[edge : edge + 1], (8, size_z))
        copies.append(
            remote(
                corner_out.at[i],
                corner_in.at[i],
                send_sem.at[6 + i],
                recv_sem.at[6 + i],
                place(way_x, way_y, 0),
            )
        )

    y_row = lax.broadcasted_iota(jnp.int32, (size_y, size_z), 0)

    def moved(q, x):
        way_x, way_y = int(lattice_dirs[q][0]), int(lattice_dirs[q][1])
        from_x = x - way_x
        outside = from_x < 0 or from_x >= size_x
        if outside:
            values = x_in[ways.index(way_x), moving(0, way_x).index(q)]
        else:
            values = block(q, from_x)
        if way_y:
            if outside:
                line = corner_in[corners.index((way_x, way_y))][0:1]
            else:
                line = y_in[ways.index(way_y), moving(1, way_y).index(q)][from_x : from_x + 1]
            edge = 0 if way_y > 0 else size_y - 1
            values = jnp.where(y_row == edge, line, pltpu.roll(values, way_y % size_y, 0))
        return values

    def inner(q, x):
        way_x, way_y = int(lattice_dirs[q][0]), int(lattice_dirs[q][1])
        return way_y == 0 and (way_x == 0 or 0 < x < size_x - 1)

    for early in (True, False):
        if not early:
            for copy in copies:
                copy.wait()
        for x in range(size_x):
            rows = pl.ds(x * size_y, size_y)
            wall = solid_ref[rows] > 0
            if early:
                fluid_ref[0, rows] = moved(0, x)
            for q in range(1, directions, 2):
                if inner(q, x) != early:
                    continue
                here, there = moved(q, x), moved(q + 1, x)
                fluid_ref[q, rows] = jnp.where(wall, there, here)
                fluid_ref[q + 1, rows] = jnp.where(wall, here, there)

    for copy in slab_copies:
        copy.wait()
    slab = lax.axis_index("gy")
    added = slab_in[slab]
    for j in range(1, count_y):
        added = added + slab_in[lax.rem(slab - j + count_y, count_y)]
    values = state_ref[...]
    after = advance_rows([values[i : i + 1] for i in range(18)], [added[i : i + 1] for i in range(6)])
    for i in range(18):
        next_ref[i : i + 1] = after[i]


def exchange(owners, count_y, size_y, post, solid, loads, state):
    directions, plane, size_z = post.shape
    size_x = plane // size_y
    vmem = pl.BlockSpec(memory_space=pltpu.VMEM)
    sides = len(moving(0, 1))
    dma = pltpu.SemaphoreType.DMA
    return pl.pallas_call(
        functools.partial(exchange_kernel, owners, count_y, size_y),
        out_shape=(jax.ShapeDtypeStruct(post.shape, f32), jax.ShapeDtypeStruct(state.shape, f32)),
        in_specs=[vmem] * 4,
        out_specs=(vmem, vmem),
        scratch_shapes=[
            pltpu.VMEM((2 * sides, plane, size_z), f32),
            pltpu.VMEM((2, plane, size_z), f32),
            pltpu.VMEM((2, plane, size_z), f32),
            pltpu.VMEM((2, sides, size_y, size_z), f32),
            pltpu.VMEM((2, sides, size_y, size_z), f32),
            pltpu.VMEM((2, sides, size_x, size_z), f32),
            pltpu.VMEM((2, sides, size_x, size_z), f32),
            pltpu.VMEM((4, 8, size_z), f32),
            pltpu.VMEM((4, 8, size_z), f32),
            pltpu.VMEM((owners,) + loads.shape, f32),
            pltpu.VMEM(loads.shape, f32),
            pltpu.VMEM((count_y,) + loads.shape, f32),
            dma((10,)),
            dma((10,)),
            dma((owners,)),
            dma((owners,)),
            dma((count_y,)),
            dma((count_y,)),
        ],
        compiler_params=pltpu.CompilerParams(
            collective_id=1, has_side_effects=True, vmem_limit_bytes=40 * 1024 * 1024
        ),
    )(post, solid, loads, state)


def columns(matrix, count):
    return [matrix[:, i : i + 1] for i in range(count)]


def lane_pack(values):
    rows = values[0].shape[0]
    lane = lax.broadcasted_iota(jnp.int32, (rows, 128), 1)
    out = jnp.zeros((rows, 128), f32)
    for i, value in enumerate(values):
        out = jnp.where(lane == i, value, out)
    return out


def total(values):
    return jnp.sum(values, axis=1, keepdims=True)


def step_kernel(
    size_y,
    tile_cap,
    owned,
    chunk,
    group,
    pick_ref,
    state_ref,
    slots_ref,
    contacts_ref,
    holder_ref,
    coef_ref,
    fluid_ref,
    solid_ref,
    post_ref,
    loads_ref,
    poly_ref,
    level_ref,
    grid_ref,
    speed_ref,
    force_ref,
    cell_ref,
    velocity_ref,
):
    state = state_ref[...]
    grains = state.shape[1]
    tile_slots, _, nodes = slots_ref.shape
    contact_slots = contacts_ref.shape[0]
    order = coef_ref.shape[1]
    directions, plane, size_z = fluid_ref.shape
    size_x = plane // size_y

    def one_hot(ids):
        lane = lax.broadcasted_iota(jnp.int32, (ids.shape[0], grains), 1).astype(f32)
        return jnp.where(lane == ids, 1.0, 0.0)

    def named(tiles_ref, per_source):
        ids = tiles_ref[:, 7, :][:, 0:1]
        source = lax.broadcasted_iota(jnp.int32, ids.shape, 0).astype(f32)
        source = jnp.floor((source + 0.5) * (1.0 / per_source))
        return jnp.where(ids >= 0.0, ids + source * owned, -1.0)

    def picked(hot):
        found = lax.dot_general(
            hot, state, (((1,), (1,)), ((), ())), precision=highest, preferred_element_type=f32
        )
        return columns(found, 18)

    def gathered(values, hot):
        return lax.dot_general(
            lane_pack(values), hot, (((0,), (0,)), ((), ())), precision=highest, preferred_element_type=f32
        )[0:8]

    partner_hot = one_hot(named(contacts_ref, contact_slots // (tile_slots // tile_cap)))
    holder_hot = one_hot(holder_ref[...])
    partner = picked(partner_hot)
    holder = picked(holder_hot)
    alive = jnp.where(holder_ref[...] >= 0.0, 1.0, 0.0)
    body = [contacts_ref[:, i, :] for i in range(3)]
    arm = [
        partner[3 * i] * body[0] + partner[3 * i + 1] * body[1] + partner[3 * i + 2] * body[2]
        for i in range(3)
    ]
    rel = [(partner[9 + i] + arm[i]) - holder[9 + i] for i in range(3)]
    for d in range(3):
        y = jnp.clip(holder[d] * rel[0] + holder[3 + d] * rel[1] + holder[6 + d] * rel[2], -1.0, 1.0)
        first = [jnp.ones_like(y), y]
        second = [jnp.ones_like(y), 2.0 * y]
        for degree in range(2, order):
            first.append(2.0 * y * first[-1] - first[-2])
            second.append(2.0 * y * second[-1] - second[-2])
        for degree in range(order):
            slope = degree * second[degree - 1] if degree else jnp.zeros_like(y)
            poly_ref[2 * d, :, degree, :] = first[degree]
            poly_ref[2 * d + 1, :, degree, :] = slope

    def contact(slot, carry):
        high, low = split(coef_ref[pick_ref[slot]])
        table = jnp.concatenate([high, low, high], axis=0)
        along = jnp.concatenate([poly_ref[0, slot], poly_ref[1, slot]], axis=1)
        along_high, along_low = split(along)
        along = jnp.concatenate([along_high, along_high, along_low], axis=0)
        part = lax.dot_general(table, along, (((0,), (0,)), ((), ())), preferred_element_type=f32)
        poly_y, slope_y = poly_ref[2, slot], poly_ref[3, slot]
        poly_z, slope_z = poly_ref[4, slot], poly_ref[5, slot]
        value = slope_xp = slope_yp = None
        for b in range(order):
            here = part[b * order : (b + 1) * order, 0:nodes]
            there = part[b * order : (b + 1) * order, nodes : 2 * nodes]
            t, s = poly_y[b : b + 1], slope_y[b : b + 1]
            if b == 0:
                value, slope_xp, slope_yp = here * t, there * t, here * s
            else:
                value, slope_xp, slope_yp = value + here * t, slope_xp + there * t, slope_yp + here * s
        for i, terms in enumerate((value * poly_z, slope_xp * poly_z, slope_yp * poly_z, value * slope_z)):
            level_ref[i, pl.ds(slot, 1), :] = jnp.sum(terms, axis=0, keepdims=True)
        return carry

    lax.fori_loop(0, contact_slots, contact, 0, unroll=math.gcd(contact_slots, 4))

    gradient = [level_ref[i + 1] for i in range(3)]
    depth = jnp.maximum(-level_ref[0], 0.0)
    norm = gradient[0] * gradient[0] + gradient[1] * gradient[1] + gradient[2] * gradient[2]
    strength = contact_stiffness * depth / jnp.sqrt(1.0 + norm) * alive
    push = [
        (holder[3 * i] * gradient[0] + holder[3 * i + 1] * gradient[1] + holder[3 * i + 2] * gradient[2])
        * strength
        for i in range(3)
    ]
    sums = [total(push[i]) for i in range(3)]
    on_holder = [-s for s in sums] + [-total(t) for t in cross(rel, push)]
    on_partner = sums + [total(t) for t in cross(arm, push)]
    loads = gathered(on_holder, holder_hot) + gathered(on_partner, partner_hot)

    density = fluid_ref[0]
    momentum = [None, None, None]
    for q in range(1, directions):
        values = fluid_ref[q]
        density = density + values
        for i in range(3):
            e = int(lattice_dirs[q][i])
            if e:
                term = values if e > 0 else -values
                momentum[i] = term if momentum[i] is None else momentum[i] + term
    inverse = 1.0 / density
    for i in range(3):
        flow = momentum[i] * inverse
        velocity_ref[i] = flow
        high, low = split(flow)
        rows = pl.ds(i * plane, plane)
        grid_ref[rows, 0:size_z] = high
        grid_ref[rows, size_z : 2 * size_z] = low
        grid_ref[rows, 2 * size_z : 3 * size_z] = high

    slot_hot = one_hot(named(slots_ref, tile_cap))
    own = picked(slot_hot)
    body = [slots_ref[:, i, :] for i in range(3)]
    arm = [own[3 * i] * body[0] + own[3 * i + 1] * body[1] + own[3 * i + 2] * body[2] for i in range(3)]
    swirl = cross(own[15:18], arm)
    for i in range(3):
        speed_ref[:, i, :] = own[12 + i] + swirl[i]
    force_ref[...] = jnp.zeros_like(force_ref)
    cell_ref[...] = jnp.zeros_like(cell_ref)
    kind = bf16 if size_z <= 256 else f32
    depth_row = lax.broadcasted_iota(jnp.int32, (size_z, nodes), 0).astype(f32).astype(kind)
    y_row = lax.broadcasted_iota(jnp.int32, (size_y, nodes), 0).astype(f32)

    def weights_of(slot):
        tile = slots_ref[slot]
        cell = tile[6:7]
        line = jnp.floor((cell + 0.5) * (1.0 / size_z))
        base_z = cell - line * size_z
        base_x = jnp.floor((line + 0.5) * (1.0 / size_y))
        base_y = line - base_x * size_y
        upper, lower = tile[5:6], 1.0 - tile[5:6]
        upper_high, upper_low = split(upper)
        lower_high, lower_low = split(lower)
        none = jnp.zeros((size_z, nodes), kind)
        at_low, at_high = depth_row == base_z.astype(kind), depth_row == (base_z + 1.0).astype(kind)

        def placed(low_value, high_value):
            far = jnp.where(at_high, high_value.astype(kind), none)
            return jnp.where(at_low, low_value.astype(kind), far).astype(bf16)

        frac_y = tile[4:5]
        weight_y = jnp.where(
            y_row == base_y, 1.0 - frac_y, jnp.where(y_row == base_y + 1.0, frac_y, 0.0)
        )
        frac_x = tile[3:4]
        rows = []
        for x in range(size_x):
            weight_x = jnp.where(
                base_x == float(x), 1.0 - frac_x, jnp.where(base_x == float(x - 1), frac_x, 0.0)
            )
            rows.append(weight_x * weight_y)
        high, low = placed(lower_high, upper_high), placed(lower_low, upper_low)
        return high, low, jnp.concatenate(rows, axis=0)

    def spread(start):
        starts = [start + part * group for part in range(chunk // group)]
        sets = [[weights_of(first + k) for k in range(group)] for first in starts]
        highs = [jnp.concatenate([w[0] for w in each], axis=1) for each in sets]
        lows = [jnp.concatenate([w[1] for w in each], axis=1) for each in sets]
        lines = [
            jnp.dot(
                grid_ref[...], jnp.concatenate([high, high, low], axis=0), preferred_element_type=f32
            )
            for high, low in zip(highs, lows)
        ]
        added = None
        contract = (((1,), (1,)), ((), ()))
        for first, each, high, low, line in zip(starts, sets, highs, lows, lines):
            spread_high, spread_low = [], []
            for k in range(group):
                weights = each[k][2]
                live = jnp.where(slots_ref[first + k][7:8] >= 0.0, ib_stiffness, 0.0)
                speed = speed_ref[first + k]
                pieces = []
                for i in range(3):
                    taken = line[i * plane : (i + 1) * plane, k * nodes : (k + 1) * nodes]
                    interp = jnp.sum(taken * weights, axis=0, keepdims=True)
                    node = live * (speed[i : i + 1] - interp)
                    force_ref[first + k, i : i + 1, :] = node
                    pieces.append(node * weights)
                piece_high, piece_low = split(jnp.concatenate(pieces, axis=0))
                spread_high.append(piece_high)
                spread_low.append(piece_low)
            wide = lax.dot_general(
                jnp.concatenate(spread_high, axis=1),
                jnp.concatenate([high, low], axis=0),
                contract,
                preferred_element_type=f32,
            )
            narrow = lax.dot_general(
                jnp.concatenate(spread_low, axis=1), high, contract, preferred_element_type=f32
            )
            term = wide[:, 0:size_z] + wide[:, size_z : 2 * size_z] + narrow
            added = term if added is None else added + term
        cell_ref[...] += added

    for source in range(tile_slots // tile_cap):

        def body_of(turn, carry, source=source):
            spread(source * tile_cap + turn * chunk)
            return carry

        ids = slots_ref[source * tile_cap : (source + 1) * tile_cap, 7, :][:, 0:1]
        count = jnp.sum(jnp.where(ids >= 0.0, 1.0, 0.0)).astype(jnp.int32)
        lax.fori_loop(0, lax.div(count + (chunk - 1), chunk), body_of, 0)

    node = [force_ref[:, i, :] for i in range(3)]
    back = [-total(node[i]) for i in range(3)] + [-total(t) for t in cross(arm, node)]
    loads_ref[...] = loads + gathered(back, slot_hot)

    for x in range(size_x):
        rows = slice(x * size_y, (x + 1) * size_y)
        density = fluid_ref[0, rows]
        for q in range(1, directions):
            density = density + fluid_ref[q, rows]
        scale = tau_relax / density
        shifted = [
            velocity_ref[i, rows] + scale * cell_ref[i * plane + x * size_y : i * plane + (x + 1) * size_y, :]
            for i in range(3)
        ]
        speed = shifted[0] * shifted[0] + shifted[1] * shifted[1] + shifted[2] * shifted[2]
        base = 1.0 - 1.5 * speed
        wall = solid_ref[rows] > 0
        for q in range(directions):
            flat = fluid_ref[q, rows]
            along = None
            for i in range(3):
                e = int(lattice_dirs[q][i])
                if e:
                    term = shifted[i] if e > 0 else -shifted[i]
                    along = term if along is None else along + term
            inside = base if along is None else base + along * (3.0 + 4.5 * along)
            balance = lattice_weights[q] * density * inside
            relaxed = flat - (flat - balance) * (1.0 / tau_relax)
            post_ref[q, rows] = jnp.where(wall, flat, relaxed)


def run_step(size_y, tile_cap, owned, pick, state, slots, contacts, holder, coefs, fluid, solid):
    grains = state.shape[1]
    tile_slots, _, nodes = slots.shape
    contact_slots = contacts.shape[0]
    order = coefs.shape[1]
    directions, plane, size_z = fluid.shape
    vmem = pl.BlockSpec(memory_space=pltpu.VMEM)
    smem = pl.BlockSpec(memory_space=pltpu.SMEM)
    return pl.pallas_call(
        functools.partial(
            step_kernel, size_y, tile_cap, owned, math.gcd(tile_cap, 8), math.gcd(tile_cap, 4)
        ),
        out_shape=(
            jax.ShapeDtypeStruct(fluid.shape, f32),
            jax.ShapeDtypeStruct((8, grains), f32),
        ),
        in_specs=[smem] + [vmem] * 7,
        out_specs=(vmem, vmem),
        scratch_shapes=[
            pltpu.VMEM((6, contact_slots, order, nodes), f32),
            pltpu.VMEM((4, contact_slots, nodes), f32),
            pltpu.VMEM((3 * plane, 3 * size_z), bf16),
            pltpu.VMEM((tile_slots, 8, nodes), f32),
            pltpu.VMEM((tile_slots, 8, nodes), f32),
            pltpu.VMEM((3 * plane, size_z), f32),
            pltpu.VMEM((3, plane, size_z), f32),
        ],
        compiler_params=pltpu.CompilerParams(vmem_limit_bytes=40 * 1024 * 1024),
    )(pick, state, slots, contacts, holder, coefs, fluid, solid)


def per_device(
    populations,
    solid,
    coefficients,
    body_nodes,
    centers,
    angles,
    velocity,
    node_frac,
    node_cell,
    grain_tile,
    send_grain,
    recv_partner,
):
    directions, size_x, size_y, size_z = populations.shape
    plane = size_x * size_y
    grains = centers.shape[1]
    nodes = body_nodes.shape[1]
    count_z = lax.axis_size("gz")
    owners = lax.axis_size("gx") * count_z
    tile_cap = max(2, 2 * grains // owners)
    tile_slots = owners * tile_cap
    contact_slots = send_grain.shape[1]
    contact_cap = contact_slots // owners
    me = lax.axis_index("gx") * count_z + lax.axis_index("gz")
    first = (me * grains).astype(f32)

    tiles = jnp.concatenate(
        [body_nodes, node_frac, node_cell.astype(f32)[None], jnp.zeros((1, nodes, grains), f32)]
    ).transpose(2, 0, 1)
    slots, contacts, small = plan(
        owners, tile_cap, grain_tile[0, :, 0], send_grain[0], tiles, angles, centers, velocity
    )
    slots, contacts, everyone = deal(slots, contacts.reshape(owners, contact_cap, 8, nodes), small)
    slots = slots.reshape(tile_slots, 8, nodes)
    contacts = contacts.reshape(contact_slots, 8, nodes)
    state = everyone[:, :18, :grains].transpose(1, 0, 2).reshape(18, owners * grains)
    recv = recv_partner[0]
    pick = jnp.maximum(recv, 0)
    holder = jnp.where(recv >= 0, recv.astype(f32) + first, -1.0)[:, None]

    solid_flat = solid.reshape(plane, size_z)
    fluid = populations.reshape(directions, plane, size_z)
    for step in range(STEPS):
        post, loads = run_step(
            size_y,
            tile_cap,
            grains,
            pick,
            state,
            slots,
            contacts,
            holder,
            coefficients,
            fluid,
            solid_flat,
        )
        fluid, state = exchange(owners, lax.axis_size("gy"), size_y, post, solid_flat, loads, state)
    state = lax.dynamic_slice(state, (9, me * grains), (9, grains))
    return (fluid.reshape(populations.shape), state[0:3], state[3:9])


def solution(mesh):
    in_specs = (
        P(None, "gx", "gy", "gz"),
        P("gx", "gy", "gz"),
        P(("gx", "gz"), None, None),
        P(None, "gy", ("gx", "gz")),
        P(None, ("gx", "gz")),
        P(None, ("gx", "gz")),
        P(None, ("gx", "gz")),
        P(None, "gy", ("gx", "gz")),
        P("gy", ("gx", "gz")),
        P("gy", ("gx", "gz"), None),
        P(("gx", "gz"), None),
        P(("gx", "gz"), None),
    )
    out_specs = (P(None, "gx", "gy", "gz"), P(None, ("gx", "gz")), P(None, ("gx", "gz")))
    return jax.shard_map(
        per_device, mesh=mesh, in_specs=in_specs, out_specs=out_specs, check_vma=False
    )
```
